512 devices in a mesh: req: 8 (over z), ctx: 4 (over x), exp: 16 (over y, core).
Axes of the slice: x: 4, y: 8, z: 8, core: 2. Of those that a mesh axis runs over, the one named last changes fastest.
Arguments:
- queries: bfloat16 [256, 6144], P(('req', 'exp')), may hold values from -25 to 25
- key_pages: bfloat16 [128, 12, 64, 1024], P(('req', 'exp'), 'ctx'), may hold values from -4 to 4
- value_pages: bfloat16 [128, 12, 64, 1024], P(('req', 'exp'), 'ctx'), may hold values from -15 to 15
- block_table: int32 [256, 8], P(('req', 'exp'), 'ctx'), may hold values from 0 to 2, as said below
- context_lengths: int32 [256], P(('req', 'exp')), may hold values from 2 to 512, as said below
- residual: bfloat16 [256, 6144], P(('req', 'exp')), may hold values from -4 to 4
- norm_gain: bfloat16 [6144], replicated, may hold values from 0.099609375 to 1.8984375
- gate_blocks: bfloat16 [16, 3072, 6144], P('exp', ('req', 'ctx')), may hold values from -0.078125 to 0.078125
- up_blocks: bfloat16 [16, 3072, 6144], P('exp', ('req', 'ctx')), may hold values from -0.078125 to 0.078125
- down_blocks: bfloat16 [16, 3072, 6144], P('exp', ('req', 'ctx')), may hold values from -0.078125 to 0.078125
- expert_routes: int32 [16, 16, 4], replicated, may hold values from 0 to 7, all different within a row; in each aligned block of 16 rows (0 to 15, 16 to 31, ..., all dimensions but the last counted through in order) at most 10 rows name the same one
- route_weights: float32 [16, 16, 4], replicated, may hold values from 0.05 to 0.5
- block_expert: int32 [16], replicated, may hold values from 0 to 7, as said below
Outputs:
- layer_out: bfloat16 [256, 6144], P(('req', 'exp'), 'ctx')
The draws below stay inside these ranges and needn't reach their ends.
Inputs may be any that keep to these rules, and one draw needn't show every extreme that they name: `context_lengths`: each group holds 1 request longer than 256 positions and the others not longer. `block_table`: entries name slots of the request group's pool on the entry's context share; the live pages of one group on one share name distinct slots; entries of pages past a request's length name arbitrary slots. `expert_routes`: among the 16 rows of one index of the first dimension no expert is named more than 10 times; a row names 4 different experts. `block_expert`: each expert belongs to exactly two blocks.
All inputs are finite; a program needn't handle non-finite values.
Results may differ from the reference program's by a relative error of at most 0.015.
Values may be sent and summed in bfloat16 or wider, within the bound.
No kernel may reach another device: no remote copies, remote signals or barrier semaphores. Data moves between devices by JAX's collectives and lax.ppermute only.
A program may use at most 128 MiB of HBM per device.

```python
import math
import jax
import jax.numpy as jnp
import numpy as np
from jax import lax

HEADS = 48
KV_HEADS = 8
HEAD_DIM = 128
D = 6144
EXPERTS = 8
TOP = 4
FF = 6144
BLOCKS = 16
FF_BLOCK = 3072
PAGE = 64
SPAN = 2
REQ_DEV = 2
POOL = 3
SPLITS = 4
COLUMNS = 16
ROWGROUPS = 8
GROUPS = 128
REQUESTS = 256
GROUP_ROWS = 16
CAP = 10
MAXCTX = 512


def page_layout(key):
    key_order, key_long, key_short, key_peak, key_slots, key_dead, key_pick, key_sign, key_power = jax.random.split(key, 9)
    order_rank = jax.vmap(lambda subkey: jax.random.permutation(subkey, REQ_DEV))(jax.random.split(key_order, GROUPS))
    longer = order_rank < REQ_DEV // 2
    long_length = jax.random.randint(key_long, (GROUPS, REQ_DEV), SPLITS * PAGE + 1, MAXCTX + 1)
    short_length = jax.random.randint(key_short, (GROUPS, REQ_DEV), 2, SPLITS * PAGE + 1)
    peak_group = jax.random.randint(key_peak, (), 0, GROUPS)
    at_peak = (jnp.arange(GROUPS)[:, None] == peak_group) & (order_rank == 0)
    lengths = jnp.where(longer, long_length, short_length)
    lengths = jnp.where(at_peak, MAXCTX, lengths).astype(jnp.int32)
    reserve = jnp.where(longer, SPAN, 1)
    offsets = jnp.cumsum(reserve, axis=1) - reserve
    slot_orders = jax.vmap(lambda subkey: jax.random.permutation(subkey, POOL))(jax.random.split(key_slots, GROUPS * SPLITS)).reshape(GROUPS, 1, SPLITS, POOL)
    slot_orders = jnp.broadcast_to(slot_orders, (GROUPS, REQ_DEV, SPLITS, POOL))
    span_index = jnp.arange(SPAN)
    is_live = span_index[None, None, :] < reserve[:, :, None]
    wanted = jnp.where(is_live, offsets[:, :, None] + span_index[None, None, :], 0)
    wanted = jnp.broadcast_to(wanted[:, :, None, :], (GROUPS, REQ_DEV, SPLITS, SPAN))
    taken = jnp.take_along_axis(slot_orders, wanted, axis=3)
    dead_slot = jax.random.randint(key_dead, (GROUPS, REQ_DEV, SPLITS, SPAN), 0, POOL)
    table = jnp.where(is_live[:, :, None, :], taken, dead_slot).reshape(REQUESTS, SPLITS * SPAN).astype(jnp.int32)
    aligned = jax.random.randint(key_pick, (REQUESTS,), 0, 6) == 0
    strength = 11 + 7 * jax.random.randint(key_power, (REQUESTS,), 0, 3)
    sign_pattern = jnp.where(jax.random.randint(key_sign, (REQUESTS, KV_HEADS * HEAD_DIM), 0, 2) == 1, 1.0, -1.0)
    return (lengths.reshape(REQUESTS), table, aligned, strength, sign_pattern)


def draw_context_lengths(key, part):
    layout = page_layout(key)
    return layout[0]


def draw_block_table(key, part):
    layout = page_layout(key)
    return layout[1]


def draw_key_pages(key, part):
    key = jax.random.fold_in(key, 3)
    page_shape = (GROUPS, SPLITS * POOL, PAGE, KV_HEADS * HEAD_DIM)
    pages = jnp.clip(jax.random.normal(key, page_shape, jnp.float32), -4.0, 4.0)
    return pages.astype(jnp.bfloat16)


def draw_queries(key, part):
    key = jax.random.fold_in(key, 4)
    query_shape = (REQUESTS, HEADS * HEAD_DIM)
    result = jnp.clip(jax.random.normal(key, query_shape, jnp.float32), -4.0, 4.0)
    return result.astype(jnp.bfloat16)


def draw_residual(key, part):
    key = jax.random.fold_in(key, 5)
    key_base, key_rows, key_cols = jax.random.split(key, 3)
    base_draw = jnp.clip(jax.random.normal(key_base, (REQUESTS, D), jnp.float32), -4.0, 4.0)
    row_scale = jnp.exp(jax.random.uniform(key_rows, (REQUESTS, 1), jnp.float32, 0.0, math.log(10.0)))
    column_scale = jnp.exp(jax.random.uniform(key_cols, (1, D), jnp.float32, 0.0, math.log(10.0)))
    return (0.01 * base_draw * row_scale * column_scale).astype(jnp.bfloat16)


def draw_block_expert(key, part):
    key = jax.random.fold_in(key, 6)
    return (jax.random.permutation(key, BLOCKS) // 2).astype(jnp.int32)


def block_levels(own_key, extent, shards, smallest, largest):
    level = 1.0
    for position, parts in shards:
        heights = jax.random.uniform(jax.random.fold_in(jax.random.fold_in(own_key, 6), position), (parts,), jnp.float32, smallest / len(shards), largest / len(shards))
        level = level * jnp.repeat(jnp.exp(heights), extent[position] // parts).reshape((-1,) + (1,) * (len(extent) - 1 - position))
    return level


def deal_out(rng, own, number, rows, count, top, limit, slope):
    ranking = jax.random.permutation(rng, count)
    packed, common = load_shares(count, rows * top, limit, slope, True), load_shares(count, rows * top, limit, slope, False)
    places = jnp.arange(count)

    def named(tallies, offset_by):
        used = int((tallies > 0).sum())
        fixed = max(1, used // 4)
        moved = fixed + (places - fixed + offset_by * (used - fixed)) % max(1, count - fixed)
        return jnp.zeros((count,), jnp.int32).at[ranking[jnp.where(places < fixed, places, moved)]].set(jnp.asarray(tallies, jnp.int32))

    tallies = jnp.where(number % 4 == 0, named(packed, number // 4), named(common, number - number // 4 - 1))
    mixed = jax.random.permutation(jax.random.fold_in(own, 3), count)
    giver, receiver = mixed[0:count // 2 * 2:2], mixed[1:count // 2 * 2:2]
    slack = jnp.minimum(tallies[giver] - 1, limit - tallies[receiver]) // 2
    slack = jnp.where((giver == ranking[0]) | (receiver == ranking[0]) | (tallies[receiver] == 0), 0, jnp.maximum(slack, 0))
    moved = jax.random.randint(jax.random.fold_in(own, 4), (count // 2,), 0, 1 << 20) % (slack + 1)
    tallies = tallies.at[giver].add(-moved).at[receiver].add(moved)
    labels = jnp.searchsorted(jnp.cumsum(tallies), jnp.arange(rows * top), side="right").astype(jnp.int32)
    grid = labels.reshape(top, rows).T
    grid = grid[jax.random.permutation(jax.random.fold_in(own, 1), rows)]
    offset_by = jax.random.randint(jax.random.fold_in(own, 2), (rows, 1), 0, top)
    return jnp.take_along_axis(grid, (jnp.arange(top)[None, :] + offset_by) % top, axis=1)


def load_shares(amount, total, most, skew, full):
    portions = [(1 << 20) // math.isqrt(rank ** skew) + 1 for rank in range(1, amount + 1)]
    largest = most if full else min(most, max(-(-total // amount), total * portions[0] // sum(portions)))
    least = 1 if total - largest >= amount - 1 else 0
    counts, spare = [largest] + [least] * (amount - 1), total - largest - least * (amount - 1)
    while spare > 0:
        free = [i for i in range(1, amount) if counts[i] < largest] or [i for i in range(1, amount) if counts[i] < most]
        whole, budget = sum([portions[i] for i in free]), spare
        for i in free:
            addition = min(most - counts[i], max(1, budget * portions[i] // whole), spare)
            counts[i] = counts[i] + addition
            spare = spare - addition
    return np.array(counts)


def bell_draw(rng, dims, deviation, reach, shards=(), kind=jnp.bfloat16):
    entries = deviation * jax.random.normal(rng, dims, jnp.float32)
    if shards:
        entries = entries * block_levels(rng, dims, shards, -0.22, 0.18)
    return jnp.clip(entries, -reach, reach).astype(kind)


def setup_inputs(seed: int = 0) -> dict:
    seeds = jax.random.split(jax.random.key(seed), 14)
    queries = draw_queries(jax.random.fold_in(seeds[13], 71), 0)
    key_pages = draw_key_pages(jax.random.fold_in(seeds[13], 71), 0)
    value_pages = bell_draw(seeds[2], (GROUPS, SPLITS * POOL, PAGE, KV_HEADS * HEAD_DIM), 3.0, 15.0, ((0, 128), (1, 4)))
    block_table = draw_block_table(jax.random.fold_in(seeds[13], 71), 0)
    context_lengths = draw_context_lengths(jax.random.fold_in(seeds[13], 71), 0)
    residual = draw_residual(jax.random.fold_in(seeds[13], 71), 0)
    norm_gain = jnp.clip(1.0 + 0.18 * jax.random.normal(seeds[6], (D,), jnp.float32), 0.099609375, 1.8984375).astype(jnp.bfloat16)
    gate_blocks = bell_draw(seeds[7], (BLOCKS, FF_BLOCK, D), D ** -0.5, 0.078125, ((0, 16), (1, 32)))
    up_blocks = bell_draw(seeds[8], (BLOCKS, FF_BLOCK, D), D ** -0.5, 0.078125, ((0, 16), (1, 32)))
    down_blocks = bell_draw(seeds[9], (BLOCKS, FF_BLOCK, D), FF ** -0.5, 0.078125, ((0, 16), (1, 32)))
    expert_routes_keys = jax.random.split(jax.random.fold_in(seeds[10], 1), COLUMNS * GROUP_ROWS // GROUP_ROWS)
    expert_routes_turns = jax.random.permutation(jax.random.fold_in(seeds[10], 3), COLUMNS * GROUP_ROWS // GROUP_ROWS)
    expert_routes = jax.vmap(lambda own, number: deal_out(jax.random.fold_in(seeds[10], 2), own, number, GROUP_ROWS, EXPERTS, TOP, CAP, 2))(expert_routes_keys, expert_routes_turns).reshape((COLUMNS, GROUP_ROWS, TOP))
    route_weights = jnp.clip(jnp.exp(jax.random.uniform(seeds[11], (COLUMNS, GROUP_ROWS, TOP), jnp.float32, math.log(0.05), math.log(0.5))), 0.05, 0.5)
    block_expert = draw_block_expert(jax.random.fold_in(seeds[13], 71), 0)
    return {"queries": queries, "key_pages": key_pages, "value_pages": value_pages, "block_table": block_table, "context_lengths": context_lengths, "residual": residual, "norm_gain": norm_gain, "gate_blocks": gate_blocks, "up_blocks": up_blocks, "down_blocks": down_blocks, "expert_routes": expert_routes, "route_weights": route_weights, "block_expert": block_expert}


EPSILON = 1e-05
NEGATIVE = -1e+30

def request_attention(request, queries, key_pages, value_pages, block_table, context_lengths):
    group_id = request // REQ_DEV
    page_table = block_table[request].reshape(SPLITS, SPAN)
    pool_index = (jnp.arange(SPLITS, dtype=jnp.int32)[:, None] * POOL + page_table).astype(jnp.int32)
    cached_keys = key_pages[group_id][pool_index].reshape(SPLITS * SPAN * PAGE, KV_HEADS, HEAD_DIM)
    cached_values = value_pages[group_id][pool_index].reshape(SPLITS * SPAN * PAGE, KV_HEADS, HEAD_DIM)
    logical = jnp.arange(SPAN, dtype=jnp.int32)[None, :, None] * SPLITS + jnp.arange(SPLITS, dtype=jnp.int32)[:, None, None]
    positions = (logical * PAGE + jnp.arange(PAGE, dtype=jnp.int32)[None, None, :]).reshape(-1)
    is_live = positions < context_lengths[request]
    grouped_query = queries[request].reshape(KV_HEADS, HEADS // KV_HEADS, HEAD_DIM).astype(jnp.float32)
    scores = jnp.einsum('kgd,nkd->kgn', grouped_query, cached_keys.astype(jnp.float32)) * HEAD_DIM ** (-0.5)
    scores = jnp.where(is_live, scores, NEGATIVE)
    top_score = lax.optimization_barrier(jnp.max(scores, axis=-1, keepdims=True))
    weights = jnp.where(is_live, jnp.exp(scores - top_score), 0.0)
    weight_sum = lax.optimization_barrier(jnp.sum(weights, axis=-1))
    head_mixes = jnp.einsum('kgn,nkd->kgd', weights, cached_values.astype(jnp.float32), precision=lax.Precision.HIGHEST)
    return (head_mixes / weight_sum[..., None]).reshape(HEADS * HEAD_DIM)

def reference(queries, key_pages, value_pages, block_table, context_lengths, residual, norm_gain, gate_blocks, up_blocks, down_blocks, expert_routes, route_weights, block_expert):
    attention = lax.map(lambda request: request_attention(request, queries, key_pages, value_pages, block_table, context_lengths), jnp.arange(REQUESTS, dtype=jnp.int32))
    stream = (residual.astype(jnp.float32) + attention).astype(jnp.bfloat16)
    stream_wide = stream.astype(jnp.float32)
    normed = (stream_wide * lax.rsqrt(lax.optimization_barrier(jnp.mean(stream_wide * stream_wide, axis=-1, keepdims=True)) + EPSILON) * norm_gain.astype(jnp.float32)).astype(jnp.bfloat16)
    routes = expert_routes.reshape(COLUMNS, ROWGROUPS, REQ_DEV, TOP).transpose(1, 0, 2, 3).reshape(REQUESTS, TOP)
    route_gate = route_weights.reshape(COLUMNS, ROWGROUPS, REQ_DEV, TOP).transpose(1, 0, 2, 3).reshape(REQUESTS, TOP)
    expert_ids = jnp.arange(EXPERTS, dtype=jnp.int32)
    named_hot = (routes[:, :, None] == expert_ids).astype(jnp.float32)
    expert_weight = lax.optimization_barrier(jnp.sum(route_gate[:, :, None] * named_hot, axis=1))

    def add_block(block_id, running):
        owners = (block_expert[block_id] == expert_ids).astype(jnp.float32)
        shares = lax.optimization_barrier(jnp.sum(expert_weight * owners, axis=1))
        gate_act = jnp.dot(normed, gate_blocks[block_id].T, preferred_element_type=jnp.float32)
        up_act = jnp.dot(normed, up_blocks[block_id].T, preferred_element_type=jnp.float32)
        active = (jax.nn.silu(gate_act) * up_act).astype(jnp.bfloat16)
        block_out = jnp.dot(active, down_blocks[block_id], preferred_element_type=jnp.float32)
        return running + shares[:, None] * block_out
    expert_sum = lax.fori_loop(0, BLOCKS, add_block, jnp.zeros((REQUESTS, HEADS * HEAD_DIM), jnp.float32))
    return (stream_wide + expert_sum).astype(jnp.bfloat16)
```

```python
import functools

import jax
import jax.numpy as jnp
import numpy as np
from jax import lax
from jax.experimental import pallas as pl
from jax.experimental.pallas import tpu as pltpu
from jax.sharding import PartitionSpec as P

HEADS = 48
KV_HEADS = 8
HEAD_DIM = 128
GROUP = HEADS // KV_HEADS
EPSILON = 1e-05
NEGATIVE = -1e30
ROWS = 16
LANES = 128
AXES = ("req", "ctx", "exp")
F32 = jnp.float32
BF16 = jnp.bfloat16


def exchange_groups(n_req, n_ctx, n_exp):
    cols = n_exp // 2

    def device(z, x, y, core):
        z, x, y = (z + core) % n_req, (x + core) % n_ctx, (y + core) % cols
        return (z * n_ctx + x) * n_exp + y * 2 + core

    near = [
        [
            device(2 * zh + zl, 2 * xh + xl, 2 * yh + yl, core)
            for xl in (0, 1)
            for zl in (0, 1)
            for yl in (0, 1)
        ]
        for core in (0, 1)
        for xh in range(n_ctx // 2)
        for zh in range(n_req // 2)
        for yh in range(cols // 2)
    ]
    far = [
        [
            device(2 * zh + zl, 2 * xh + xl, 2 * yh + yl, core)
            for xh in range(n_ctx // 2)
            for zh in range(n_req // 2)
            for yh in range(cols // 2)
        ]
        for core in (0, 1)
        for xl in (0, 1)
        for zl in (0, 1)
        for yl in (0, 1)
    ]
    return near, far


def attention_kernel(n_ctx, table, lengths, place, q_ref, k_ref, v_ref, out_ref, heads):
    requests, slots, page_rows = q_ref.shape[0], k_ref.shape[1], k_ref.shape[2]
    span = table.shape[1]
    positions = slots * page_rows
    heads[...] = jnp.zeros_like(heads)
    queries = q_ref[...].astype(F32)
    for r in range(requests):
        for h in range(HEADS):
            row = (h // GROUP) * ROWS + r * GROUP + h % GROUP
            heads[row : row + 1, :] = queries[r : r + 1, h * HEAD_DIM : (h + 1) * HEAD_DIM]
    at = lax.broadcasted_iota(jnp.int32, (ROWS, positions), 1)
    row_id = lax.broadcasted_iota(jnp.int32, (ROWS, positions), 0)
    slot, offset = at // page_rows, at % page_rows
    live = None
    for r in range(requests):
        seen = None
        for s in range(span):
            position = (s * n_ctx + place[0]) * page_rows + offset
            here = (slot == table[r, s]) & (position < lengths[r])
            seen = here if seen is None else seen | here
        live = seen if live is None else jnp.where(row_id < r * GROUP, live.astype(jnp.int32), seen.astype(jnp.int32)) > 0
    out_row = lax.broadcasted_iota(jnp.int32, (ROWS, LANES), 0)
    diagonal = out_row == lax.broadcasted_iota(jnp.int32, (ROWS, LANES), 1)
    keys = k_ref[0].reshape(positions, KV_HEADS * HEAD_DIM)
    values = v_ref[0].reshape(positions, KV_HEADS * HEAD_DIM)
    for k in range(KV_HEADS):
        lanes = slice(k * HEAD_DIM, (k + 1) * HEAD_DIM)
        query = heads[k * ROWS : (k + 1) * ROWS, :].astype(BF16)
        scores = lax.dot_general(
            query, keys[:, lanes], (((1,), (1,)), ((), ())), preferred_element_type=F32
        ) * HEAD_DIM ** (-0.5)
        scores = jnp.where(live, scores, NEGATIVE)
        top = jnp.max(scores, axis=1, keepdims=True)
        weights = jnp.where(live, jnp.exp(scores - top), 0.0)
        total = jnp.sum(weights, axis=1, keepdims=True)
        high = weights.astype(BF16)
        low = (weights - high.astype(F32)).astype(BF16)
        mixes = jnp.dot(
            jnp.concatenate([high, low], axis=0), values[:, lanes], preferred_element_type=F32
        )
        mixes = mixes[:ROWS] + mixes[ROWS:]
        top_row = jnp.sum(jnp.where(diagonal, top, 0.0), axis=0, keepdims=True)
        total_row = jnp.sum(jnp.where(diagonal, total, 0.0), axis=0, keepdims=True)
        used = requests * GROUP
        out_ref[k] = jnp.where(
            out_row < used, mixes, jnp.where(out_row == used, top_row, total_row)
        )


def attention_parts(queries, key_pages, value_pages, block_table, lengths, place, n_ctx):
    smem = pl.BlockSpec(memory_space=pltpu.SMEM)
    vmem = pl.BlockSpec(memory_space=pltpu.VMEM)
    return pl.pallas_call(
        functools.partial(attention_kernel, n_ctx),
        out_shape=jax.ShapeDtypeStruct((KV_HEADS, ROWS, HEAD_DIM), F32),
        in_specs=[smem, smem, smem, vmem, vmem, vmem],
        out_specs=vmem,
        scratch_shapes=[pltpu.VMEM((KV_HEADS * ROWS, HEAD_DIM), F32)],
        name="attention_parts",
    )(block_table, lengths, place, queries, key_pages, value_pages)


def merge_kernel(place, parts_ref, residual_ref, gain_ref, piece_ref, stream_ref, merged):
    n_src, kv_here = parts_ref.shape[0], parts_ref.shape[1]
    requests, width = stream_ref.shape
    used = requests * GROUP
    diagonal = lax.broadcasted_iota(jnp.int32, (ROWS, LANES), 0) == lax.broadcasted_iota(
        jnp.int32, (ROWS, LANES), 1
    )

    def column(row):
        return jnp.sum(jnp.where(diagonal, row, 0.0), axis=1, keepdims=True)

    for k in range(kv_here):
        tops = [column(parts_ref[s, k, used : used + 1, :]) for s in range(n_src)]
        totals = [column(parts_ref[s, k, used + 1 : used + 2, :]) for s in range(n_src)]
        top = functools.reduce(jnp.maximum, tops)
        scales = [jnp.exp(t - top) for t in tops]
        mixes = sum(parts_ref[s, k] * scales[s] for s in range(n_src))
        total = sum(totals[s] * scales[s] for s in range(n_src))
        mixes = mixes / total
        for r in range(requests):
            for g in range(GROUP):
                at = (k * GROUP + g) * HEAD_DIM
                merged[r : r + 1, at : at + HEAD_DIM] = mixes[r * GROUP + g : r * GROUP + g + 1, :]
    columns = pl.ds(pl.multiple_of(place[0] * width, width), width)
    stream = (residual_ref[:, columns].astype(F32) + merged[...]).astype(BF16)
    stream_ref[...] = stream
    wide = stream.astype(F32)
    piece_ref[:, :width] = (wide * gain_ref[:, columns].astype(F32)).astype(BF16)
    square = jnp.sum(wide * wide, axis=1, keepdims=True)
    first = square.astype(BF16).astype(F32)
    second = (square - first).astype(BF16).astype(F32)
    third = square - first - second
    lane = lax.broadcasted_iota(jnp.int32, (requests, LANES), 1)
    spread = jnp.where(
        lane == 0, first, jnp.where(lane == 1, second, jnp.where(lane == 2, third, 0.0))
    )
    piece_ref[:, width:] = spread.astype(BF16)


def merge_parts(parts, residual, gain, place, width):
    requests = residual.shape[0]
    smem = pl.BlockSpec(memory_space=pltpu.SMEM)
    vmem = pl.BlockSpec(memory_space=pltpu.VMEM)
    return pl.pallas_call(
        merge_kernel,
        out_shape=(
            jax.ShapeDtypeStruct((requests, width + LANES), BF16),
            jax.ShapeDtypeStruct((requests, width), BF16),
        ),
        in_specs=[smem, vmem, vmem, vmem],
        out_specs=(vmem, vmem),
        scratch_shapes=[pltpu.VMEM((requests, width), F32)],
        name="merge_parts",
    )(place, parts, residual, gain)


def expert_kernel(
    model_width,
    core,
    tokens_ref,
    shares_ref,
    gate_a,
    gate_b,
    up_a,
    up_b,
    down_a,
    down_b,
    out_ref,
    gates,
    ups,
    squares,
    active,
):
    step = pl.program_id(0)
    chunks = pl.num_programs(0) // 2
    rows, width = gates.shape[1], gate_a.shape[2]

    @pl.when(step == 0)
    def _():
        gates[...] = jnp.zeros_like(gates)
        ups[...] = jnp.zeros_like(ups)
        squares[...] = jnp.zeros_like(squares)

    @pl.when(step < chunks)
    def _():
        tokens = tokens_ref[0, :, 0].reshape(rows, width + LANES)
        squares[...] += tokens[:, width:].astype(F32)
        tokens = tokens[:, :width]
        for b, (gate, up) in enumerate(((gate_a, up_a), (gate_b, up_b))):
            contract = (((1,), (1,)), ((), ()))
            gates[b] += lax.dot_general(tokens, gate[0], contract, preferred_element_type=F32)
            ups[b] += lax.dot_general(tokens, up[0], contract, preferred_element_type=F32)

    @pl.when(step == chunks - 1)
    def _():
        square = jnp.sum(squares[...], axis=1, keepdims=True)
        scale = lax.rsqrt(square / model_width + EPSILON)
        for b in range(2):
            gate, up = gates[b] * scale, ups[b] * scale
            silu = gate / (1.0 + jnp.exp(-gate))
            active[b] = (silu * up * shares_ref[:, b : b + 1]).astype(BF16)

    @pl.when(step >= chunks)
    def _():
        total = jnp.dot(active[0], down_a[0], preferred_element_type=F32) + jnp.dot(
            active[1], down_b[0], preferred_element_type=F32
        )
        out_ref[0, :, 0] = total.astype(BF16).reshape(out_ref.shape[1], out_ref.shape[3], width)


def expert_partials(tokens, shares, weights, core, n_ctx):
    n_xl, quarters, n_xh, far_rows, padded = tokens.shape
    width = padded - LANES
    rows = quarters * far_rows
    hidden = weights[0].shape[1]

    def first(i):
        return jnp.minimum(i, n_ctx - 1)

    def second(i):
        return jnp.maximum(i - n_ctx, 0)

    def owner(step, core):
        return lax.rem((step % n_xh) * 2 + step // n_xh + core[0], n_ctx)

    def token_block(i, core):
        return (first(i) // n_xh, 0, first(i) % n_xh, 0, 0)

    def wide_block(i, core):
        return (0, 0, owner(first(i), core))

    def down_block(i, core):
        return (0, 0, owner(second(i), core))

    def out_block(i, core):
        return (second(i) // n_xh, 0, second(i) % n_xh, 0, 0)

    weight_shape = (1, hidden, width)
    flops = 6 * rows * 2 * hidden * width * n_ctx
    return pl.pallas_call(
        functools.partial(expert_kernel, float(width * n_ctx)),
        out_shape=jax.ShapeDtypeStruct((n_xl, quarters, n_xh, far_rows, width), BF16),
        grid_spec=pltpu.PrefetchScalarGridSpec(
            num_scalar_prefetch=1,
            grid=(2 * n_ctx,),
            in_specs=[
                pl.BlockSpec((1, quarters, 1, far_rows, padded), token_block),
                pl.BlockSpec((rows, 2), lambda i, core: (0, 0)),
            ]
            + [pl.BlockSpec(weight_shape, wide_block)] * 4
            + [pl.BlockSpec(weight_shape, down_block)] * 2,
            out_specs=pl.BlockSpec((1, quarters, 1, far_rows, width), out_block),
            scratch_shapes=[
                pltpu.VMEM((2, rows, hidden), F32),
                pltpu.VMEM((2, rows, hidden), F32),
                pltpu.VMEM((rows, LANES), F32),
                pltpu.VMEM((2, rows, hidden), BF16),
            ],
        ),
        cost_estimate=pl.CostEstimate(
            flops=flops, bytes_accessed=12 * hidden * width * n_ctx, transcendentals=0
        ),
        name="expert_partials",
    )(core, tokens, shares, *weights)


def row_shares(expert_routes, route_weights, block_expert, exp_index, core, n_req):
    cols = expert_routes.shape[0] // 2
    requests = expert_routes.shape[1] // n_req

    def own(routes):
        return lax.dynamic_index_in_dim(
            routes.reshape((cols, 2) + routes.shape[1:]), core, 1, keepdims=False
        )

    routes, gate = own(expert_routes), own(route_weights)
    blocks = jnp.stack([block_expert[exp_index], block_expert[exp_index ^ 1]])
    shares = jnp.sum(
        jnp.where(routes[..., None] == blocks, gate[..., None], 0.0), axis=2
    ).reshape(cols, n_req, requests, 2)
    shares = jnp.where(core > 0, jnp.roll(shares, (-1, -1), (0, 1)), shares)
    shares = shares.reshape(cols // 2, 2, n_req // 2, 2, requests, 2)
    return shares.transpose(3, 1, 2, 0, 4, 5).reshape(-1, 2)


def on_device(
    groups,
    queries,
    key_pages,
    value_pages,
    block_table,
    context_lengths,
    residual,
    norm_gain,
    gate_blocks,
    up_blocks,
    down_blocks,
    expert_routes,
    route_weights,
    block_expert,
):
    near, far = groups
    n_req, n_ctx, n_exp = (lax.axis_size(a) for a in AXES)
    requests, model_width = queries.shape
    width = model_width // n_ctx
    place = lax.axis_index("ctx")
    exp_index = lax.axis_index("exp")
    core = exp_index % 2
    n_near, n_far = len(near[0]), len(far[0])
    far_rows = n_far // 2 * requests

    swap = [(i, i ^ 1) for i in range(n_exp)]
    gate_other, up_other, down_other = (
        lax.ppermute(w, "exp", swap) for w in (gate_blocks, up_blocks, down_blocks)
    )
    shares = row_shares(expert_routes, route_weights, block_expert, exp_index, core, n_req)

    parts = attention_parts(
        queries, key_pages, value_pages, block_table, context_lengths, place[None], n_ctx
    )
    parts = parts.reshape(n_ctx, KV_HEADS // n_ctx, ROWS, HEAD_DIM)
    parts = lax.all_to_all(parts, "ctx", 0, 0, tiled=True)
    piece, stream = merge_parts(
        parts, residual, norm_gain.reshape(1, model_width), place[None], width
    )

    def exchange(x, groups):
        return lax.all_to_all(x, AXES, 0, 0, axis_index_groups=groups, tiled=True)

    tokens = exchange(jnp.broadcast_to(piece, (n_far,) + piece.shape), far)
    tokens = tokens.reshape(2, far_rows, width + LANES)
    tokens = exchange(jnp.broadcast_to(tokens, (n_near,) + tokens.shape), near)
    tokens = tokens.reshape(2, n_near // 2, 2, far_rows, width + LANES)
    partials = expert_partials(
        tokens,
        shares,
        (gate_blocks, gate_other, up_blocks, up_other, down_blocks, down_other),
        core[None],
        n_ctx,
    )
    partials = exchange(partials.reshape(n_near, 2, far_rows, width), near)
    partials = jnp.sum(partials.astype(F32), axis=0).astype(BF16)
    partials = exchange(partials.reshape(n_far, requests, width), far)
    expert_sum = jnp.sum(partials.astype(F32), axis=0)
    return (stream.astype(F32) + expert_sum).astype(BF16)


def solution(mesh):
    in_specs = (
        P(("req", "exp"), None),
        P(("req", "exp"), "ctx", None, None),
        P(("req", "exp"), "ctx", None, None),
        P(("req", "exp"), "ctx"),
        P(("req", "exp")),
        P(("req", "exp"), None),
        P(),
        P("exp", ("req", "ctx"), None),
        P("exp", ("req", "ctx"), None),
        P("exp", ("req", "ctx"), None),
        P(),
        P(),
        P(),
    )
    out_specs = P(("req", "exp"), "ctx")
    groups = exchange_groups(*(mesh.shape[a] for a in AXES))
    return jax.shard_map(
        functools.partial(on_device, groups),
        mesh=mesh,
        in_specs=in_specs,
        out_specs=out_specs,
        check_vma=False,
    )
```

```python
import functools

import jax
import jax.numpy as jnp
import numpy as np
from jax import lax
from jax.experimental import pallas as pl
from jax.experimental.pallas import tpu as pltpu
from jax.sharding import PartitionSpec as P

HEADS = 48
KV_HEADS = 8
HEAD_DIM = 128
GROUP = HEADS // KV_HEADS
EPSILON = 1e-05
NEGATIVE = -1e30
ROWS = 16
LANES = 128
KERNEL_VMEM = 16 << 20
AXES = ("req", "ctx", "exp")
F32 = jnp.float32
BF16 = jnp.bfloat16


def in_vmem(x):
    return pltpu.with_memory_space_constraint(x, pltpu.VMEM)


def in_hbm(x):
    return pltpu.with_memory_space_constraint(x, pltpu.HBM)


def exchange_groups(n_req, n_ctx, n_exp):
    cols = n_exp // 2

    def device(z, x, y, core):
        z, x, y = (z + core) % n_req, (x + core) % n_ctx, (y + core) % cols
        return (z * n_ctx + x) * n_exp + y * 2 + core

    near = [
        [
            device(2 * zh + zl, 2 * xh + xl, 2 * yh + yl, core)
            for xl in (0, 1)
            for zl in (0, 1)
            for yl in (0, 1)
        ]
        for core in (0, 1)
        for xh in range(n_ctx // 2)
        for zh in range(n_req // 2)
        for yh in range(cols // 2)
    ]
    far = [
        [
            device(2 * zh + zl, 2 * xh + xl, 2 * yh + yl, core)
            for xh in range(n_ctx // 2)
            for zh in range(n_req // 2)
            for yh in range(cols // 2)
        ]
        for core in (0, 1)
        for xl in (0, 1)
        for zl in (0, 1)
        for yl in (0, 1)
    ]
    return near, far


def attention_kernel(
    n_ctx, table, lengths, place, q_ref, k_ref, v_ref, residual_ref, out_ref, own_ref, heads
):
    width = own_ref.shape[1]
    own_ref[...] = residual_ref[:, pl.ds(pl.multiple_of(place[0] * width, width), width)]
    requests, slots, page_rows = q_ref.shape[0], k_ref.shape[1], k_ref.shape[2]
    span = table.shape[1]
    positions = slots * page_rows
    heads[...] = jnp.zeros_like(heads)
    queries = q_ref[...].astype(F32)
    for r in range(requests):
        for h in range(HEADS):
            row = (h // GROUP) * ROWS + r * GROUP + h % GROUP
            heads[row : row + 1, :] = queries[r : r + 1, h * HEAD_DIM : (h + 1) * HEAD_DIM]
    at = lax.broadcasted_iota(jnp.int32, (ROWS, positions), 1)
    row_id = lax.broadcasted_iota(jnp.int32, (ROWS, positions), 0)
    slot, offset = at // page_rows, at % page_rows
    live = None
    for r in range(requests):
        seen = None
        for s in range(span):
            position = (s * n_ctx + place[0]) * page_rows + offset
            here = (slot == table[r, s]) & (position < lengths[r])
            seen = here if seen is None else seen | here
        live = seen if live is None else jnp.where(row_id < r * GROUP, live.astype(jnp.int32), seen.astype(jnp.int32)) > 0
    out_row = lax.broadcasted_iota(jnp.int32, (ROWS, LANES), 0)
    diagonal = out_row == lax.broadcasted_iota(jnp.int32, (ROWS, LANES), 1)
    live = jnp.concatenate([live] * KV_HEADS, axis=0)
    keys = k_ref[0].reshape(positions, KV_HEADS * HEAD_DIM)
    values = v_ref[0].reshape(positions, KV_HEADS * HEAD_DIM)
    query = heads[...].astype(BF16)

    def rows(k):
        return slice(k * ROWS, (k + 1) * ROWS)

    def lanes(k):
        return slice(k * HEAD_DIM, (k + 1) * HEAD_DIM)

    scores = jnp.concatenate(
        [
            lax.dot_general(
                query[rows(k)],
                keys[:, lanes(k)],
                (((1,), (1,)), ((), ())),
                preferred_element_type=F32,
            )
            for k in range(KV_HEADS)
        ],
        axis=0,
    )
    scores = jnp.where(live, scores * HEAD_DIM ** (-0.5), NEGATIVE)
    top = jnp.max(scores, axis=1, keepdims=True)
    weights = jnp.where(live, jnp.exp(scores - top), 0.0)
    total = jnp.sum(weights, axis=1, keepdims=True)
    high = weights.astype(BF16)
    low = (weights - high.astype(F32)).astype(BF16)
    used = requests * GROUP
    for k in range(KV_HEADS):
        mixes = jnp.dot(
            jnp.concatenate([high[rows(k)], low[rows(k)]], axis=0),
            values[:, lanes(k)],
            preferred_element_type=F32,
        )
        mixes = mixes[:ROWS] + mixes[ROWS:]
        top_row = jnp.sum(jnp.where(diagonal, top[rows(k)], 0.0), axis=0, keepdims=True)
        total_row = jnp.sum(jnp.where(diagonal, total[rows(k)], 0.0), axis=0, keepdims=True)
        out_ref[k] = jnp.where(
            out_row < used, mixes, jnp.where(out_row == used, top_row, total_row)
        )


def attention_parts(
    queries, key_pages, value_pages, block_table, lengths, residual, place, n_ctx
):
    smem = pl.BlockSpec(memory_space=pltpu.SMEM)
    vmem = pl.BlockSpec(memory_space=pltpu.VMEM)
    return pl.pallas_call(
        functools.partial(attention_kernel, n_ctx),
        out_shape=(
            pltpu.VMEM((KV_HEADS, ROWS, HEAD_DIM), F32),
            pltpu.VMEM((residual.shape[0], residual.shape[1] // n_ctx), BF16),
        ),
        in_specs=[smem, smem, smem, vmem, vmem, vmem, vmem],
        out_specs=(vmem, vmem),
        scratch_shapes=[pltpu.VMEM((KV_HEADS * ROWS, HEAD_DIM), F32)],
        compiler_params=pltpu.CompilerParams(vmem_limit_bytes=KERNEL_VMEM),
        name="attention_parts",
    )(
        in_hbm(block_table),
        in_hbm(lengths),
        place,
        *(in_hbm(x) for x in (queries, key_pages, value_pages, residual)),
    )


def merge_kernel(place, parts_ref, residual_ref, gain_ref, piece_ref, stream_ref, merged):
    n_src, kv_here = parts_ref.shape[0], parts_ref.shape[1]
    requests, width = stream_ref.shape
    used = requests * GROUP
    diagonal = lax.broadcasted_iota(jnp.int32, (ROWS, LANES), 0) == lax.broadcasted_iota(
        jnp.int32, (ROWS, LANES), 1
    )

    def column(row):
        return jnp.sum(jnp.where(diagonal, row, 0.0), axis=1, keepdims=True)

    for k in range(kv_here):
        tops = [column(parts_ref[s, k, used : used + 1, :]) for s in range(n_src)]
        totals = [column(parts_ref[s, k, used + 1 : used + 2, :]) for s in range(n_src)]
        top = functools.reduce(jnp.maximum, tops)
        scales = [jnp.exp(t - top) for t in tops]
        mixes = sum(parts_ref[s, k] * scales[s] for s in range(n_src))
        total = sum(totals[s] * scales[s] for s in range(n_src))
        mixes = mixes / total
        for r in range(requests):
            for g in range(GROUP):
                at = (k * GROUP + g) * HEAD_DIM
                merged[r : r + 1, at : at + HEAD_DIM] = mixes[r * GROUP + g : r * GROUP + g + 1, :]
    columns = pl.ds(pl.multiple_of(place[0] * width, width), width)
    stream = (residual_ref[...].astype(F32) + merged[...]).astype(BF16)
    stream_ref[...] = stream
    wide = stream.astype(F32)
    scaled = (wide * gain_ref[:, columns].astype(F32)).astype(BF16)
    square = jnp.sum(wide * wide, axis=1, keepdims=True)
    first = square.astype(BF16).astype(F32)
    second = (square - first).astype(BF16).astype(F32)
    third = square - first - second
    lane = lax.broadcasted_iota(jnp.int32, (requests, LANES), 1)
    spread = jnp.where(
        lane == 0, first, jnp.where(lane == 1, second, jnp.where(lane == 2, third, 0.0))
    )
    spread = spread.astype(BF16)
    for copy in range(piece_ref.shape[0]):
        piece_ref[copy, :, :width] = scaled
        piece_ref[copy, :, width:] = spread


def merge_parts(parts, residual, gain, place, width, copies):
    requests = residual.shape[0]
    smem = pl.BlockSpec(memory_space=pltpu.SMEM)
    vmem = pl.BlockSpec(memory_space=pltpu.VMEM)
    return pl.pallas_call(
        merge_kernel,
        out_shape=(
            pltpu.VMEM((copies, requests, width + LANES), BF16),
            jax.ShapeDtypeStruct((requests, width), BF16),
        ),
        in_specs=[smem, vmem, vmem, vmem],
        out_specs=(vmem, vmem),
        scratch_shapes=[pltpu.VMEM((requests, width), F32)],
        compiler_params=pltpu.CompilerParams(vmem_limit_bytes=KERNEL_VMEM),
        name="merge_parts",
    )(place, in_vmem(parts), in_vmem(residual), gain)


def row_shares(table, blocks, core, n_req, rows):
    top, entries = table.shape[0] // 2, table.shape[1]
    per_exp = entries // (n_req * 2)
    requests = entries // per_exp // n_req
    half_z, half_y = n_req // 2, per_exp // 4
    row = lax.broadcasted_iota(jnp.int32, (entries, rows), 1)
    entry = lax.broadcasted_iota(jnp.int32, (entries, rows), 0)
    request, row = row % requests, row // requests
    yh, row = row % half_y, row // half_y
    zh, row = row % half_z, row // half_z
    yl, zl = row % 2, row // 2
    z = (2 * zh + zl + core) % n_req
    y = (2 * yh + yl + core) % (per_exp // 2)
    wanted = ((2 * y + core) * n_req + z) * requests + request
    pick = jnp.where(entry == wanted, 1.0, 0.0).astype(BF16)
    lines = []
    for block in blocks:
        named = table[:top] == block.astype(F32)
        line = jnp.sum(jnp.where(named, table[top:], 0.0), axis=0, keepdims=True)
        first = line.astype(BF16)
        second = (line - first.astype(F32)).astype(BF16)
        third = (line - first.astype(F32) - second.astype(F32)).astype(BF16)
        lines += [first, second, third]
    lines.append(jnp.zeros((16 - len(lines), entries), BF16))
    picked = jnp.dot(jnp.concatenate(lines, axis=0), pick, preferred_element_type=F32)
    return [picked[i : i + 1] + picked[i + 1 : i + 2] + picked[i + 2 : i + 3] for i in (0, 3)]


def expert_kernel(model_width, n_req, exp_index, block_expert, tokens_ref, table_ref, *refs):
    sources, out_ref, held, arrived = refs[:6], refs[6], refs[7:13], refs[13]
    copies = [
        pltpu.make_async_copy(source, here, arrived.at[i])
        for i, (source, here) in enumerate(zip(sources, held))
    ]
    for copy in copies:
        copy.start()
    n_xl, quarters, n_xh, far_rows, width = out_ref.shape
    n_ctx, rows, hidden = n_xl * n_xh, quarters * far_rows, held[0].shape[1]
    contract = (((1,), (1,)), ((), ()))
    ones = jnp.ones((8, LANES), BF16)

    own = exp_index[0]
    core = lax.rem(own, 2)
    blocks = (block_expert[own], block_expert[own + 1 - 2 * core])
    shares = row_shares(table_ref[...], blocks, core, n_req, rows)

    def at(chunk):
        column = lax.rem(chunk + n_ctx - core, n_ctx)
        return column % n_xl, column // n_xl

    def added(total, term):
        return term if total is None else total + term

    squares = None
    for chunk in range(n_ctx):
        xl, xh = at(chunk)
        tokens = tokens_ref[xl, :, xh, :, width:].reshape(rows, LANES)
        squares = added(
            squares, lax.dot_general(ones, tokens, contract, preferred_element_type=F32)
        )
    scale = lax.rsqrt(squares[:1] / model_width + EPSILON)
    active = []
    for b in range(2):
        for copy in copies[2 * b : 2 * b + 2]:
            copy.wait()
        products = None
        for chunk in range(n_ctx):
            xl, xh = at(chunk)
            tokens = tokens_ref[xl, :, xh, :, :width].reshape(rows, width)
            columns = slice(chunk * width, (chunk + 1) * width)
            wide = jnp.concatenate([w[0, :, columns] for w in held[2 * b : 2 * b + 2]], axis=0)
            products = added(
                products,
                lax.dot_general(wide, tokens, contract, preferred_element_type=F32),
            )
        gate, up = products[:hidden] * scale, products[hidden:] * scale
        active.append(gate / (1.0 + jnp.exp(-gate)) * up * shares[b])
    active.append(jnp.zeros((-2 * hidden % LANES, rows), F32))
    active = jnp.concatenate(active, axis=0).T[:, : 2 * hidden].astype(BF16)
    for copy in copies[4:]:
        copy.wait()
    for chunk in range(n_ctx):
        xl, xh = at(chunk)
        columns = slice(chunk * width, (chunk + 1) * width)
        down = jnp.concatenate([w[0, :, columns] for w in held[4:]], axis=0)
        total = jnp.dot(active, down, preferred_element_type=F32).astype(BF16)
        out_ref[xl, :, xh] = total.reshape(quarters, far_rows, width)


def routing_table(expert_routes, route_weights):
    top = expert_routes.shape[2]
    table = jnp.concatenate([expert_routes.astype(F32), route_weights], axis=2)
    return table.transpose(2, 0, 1).reshape(2 * top, -1)


def expert_partials(tokens, table, block_expert, weights, exp_index, n_req):
    n_xl, quarters, n_xh, far_rows, padded = tokens.shape
    width = padded - LANES
    rows, model_width = quarters * far_rows, width * n_xl * n_xh
    hidden = weights[0].shape[1]
    smem = pl.BlockSpec(memory_space=pltpu.SMEM)
    vmem = pl.BlockSpec(memory_space=pltpu.VMEM)
    return pl.pallas_call(
        functools.partial(expert_kernel, float(model_width), n_req),
        out_shape=pltpu.VMEM((n_xl, quarters, n_xh, far_rows, width), BF16),
        in_specs=[smem, smem, vmem, vmem]
        + [pl.BlockSpec(memory_space=pltpu.HBM)] * len(weights),
        out_specs=vmem,
        scratch_shapes=[pltpu.VMEM(w.shape, w.dtype) for w in weights]
        + [pltpu.SemaphoreType.DMA((len(weights),))],
        compiler_params=pltpu.CompilerParams(vmem_limit_bytes=KERNEL_VMEM),
        cost_estimate=pl.CostEstimate(
            flops=12 * rows * hidden * model_width,
            bytes_accessed=12 * hidden * model_width,
            transcendentals=0,
        ),
        name="expert_partials",
    )(
        exp_index, block_expert, in_vmem(tokens), in_vmem(table), *(in_hbm(w) for w in weights)
    )


def on_device(
    groups,
    queries,
    key_pages,
    value_pages,
    block_table,
    context_lengths,
    residual,
    norm_gain,
    gate_blocks,
    up_blocks,
    down_blocks,
    expert_routes,
    route_weights,
    block_expert,
):
    near, far = groups
    n_req, n_ctx, n_exp = (lax.axis_size(a) for a in AXES)
    requests, model_width = queries.shape
    width = model_width // n_ctx
    place = lax.axis_index("ctx")
    exp_index = lax.axis_index("exp")
    n_near, n_far = len(near[0]), len(far[0])
    far_rows = n_far // 2 * requests

    swap = [(i, i ^ 1) for i in range(n_exp)]
    gate_other, up_other, down_other = (
        lax.ppermute(w, "exp", swap) for w in (gate_blocks, up_blocks, down_blocks)
    )

    parts, residual = attention_parts(
        queries,
        key_pages,
        value_pages,
        block_table,
        context_lengths,
        residual,
        place[None],
        n_ctx,
    )
    parts = parts.reshape(n_ctx, KV_HEADS // n_ctx, ROWS, HEAD_DIM)
    parts = lax.all_to_all(parts, "ctx", 0, 0, tiled=True)
    piece, stream = merge_parts(
        parts, residual, norm_gain.reshape(1, model_width), place[None], width, n_far
    )

    def exchange(x, groups):
        return lax.all_to_all(x, AXES, 0, 0, axis_index_groups=groups, tiled=True)

    tokens = exchange(piece, far)
    tokens = tokens.reshape(2, far_rows, width + LANES)
    tokens = exchange(jnp.broadcast_to(tokens, (n_near,) + tokens.shape), near)
    tokens = tokens.reshape(2, n_near // 2, 2, far_rows, width + LANES)
    partials = expert_partials(
        tokens,
        routing_table(expert_routes, route_weights),
        block_expert,
        (gate_blocks, up_blocks, gate_other, up_other, down_blocks, down_other),
        exp_index[None],
        n_req,
    )
    partials = exchange(partials.reshape(n_near, 2, far_rows, width), near)
    partials = jnp.sum(partials.astype(F32), axis=0).astype(BF16)
    partials = exchange(partials.reshape(n_far, requests, width), far)
    expert_sum = jnp.sum(partials.astype(F32), axis=0)
    return (stream.astype(F32) + expert_sum).astype(BF16)


def solution(mesh):
    in_specs = (
        P(("req", "exp"), None),
        P(("req", "exp"), "ctx", None, None),
        P(("req", "exp"), "ctx", None, None),
        P(("req", "exp"), "ctx"),
        P(("req", "exp")),
        P(("req", "exp"), None),
        P(),
        P("exp", ("req", "ctx"), None),
        P("exp", ("req", "ctx"), None),
        P("exp", ("req", "ctx"), None),
        P(),
        P(),
        P(),
    )
    out_specs = P(("req", "exp"), "ctx")
    groups = exchange_groups(*(mesh.shape[a] for a in AXES))
    return jax.shard_map(
        functools.partial(on_device, groups),
        mesh=mesh,
        in_specs=in_specs,
        out_specs=out_specs,
        check_vma=False,
    )
```

```python
import functools

import jax
import jax.numpy as jnp
import numpy as np
from jax import lax
from jax.experimental import pallas as pl
from jax.experimental.pallas import tpu as pltpu
from jax.sharding import PartitionSpec as P

HEADS = 48
KV_HEADS = 8
HEAD_DIM = 128
GROUP = HEADS // KV_HEADS
EPSILON = 1e-05
NEGATIVE = -1e30
ROWS = 16
LANES = 128
KERNEL_VMEM = 16 << 20
AXES = ("req", "ctx", "exp")
F32 = jnp.float32
BF16 = jnp.bfloat16


def in_vmem(x):
    return pltpu.with_memory_space_constraint(x, pltpu.VMEM)


def in_hbm(x):
    return pltpu.with_memory_space_constraint(x, pltpu.HBM)


def exchange_groups(n_req, n_ctx, n_exp):
    cols = n_exp // 2

    def device(z, x, y, core):
        z, x, y = (z + core) % n_req, (x + core) % n_ctx, (y + core) % cols
        return (z * n_ctx + x) * n_exp + y * 2 + core

    near = [
        [
            device(2 * zh + zl, 2 * xh + xl, 2 * yh + yl, core)
            for xl in (0, 1)
            for zl in (0, 1)
            for yl in (0, 1)
        ]
        for core in (0, 1)
        for xh in range(n_ctx // 2)
        for zh in range(n_req // 2)
        for yh in range(cols // 2)
    ]
    far = [
        [
            device(2 * zh + zl, 2 * xh + xl, 2 * yh + yl, core)
            for xh in range(n_ctx // 2)
            for zh in range(n_req // 2)
            for yh in range(cols // 2)
        ]
        for core in (0, 1)
        for xl in (0, 1)
        for zl in (0, 1)
        for yl in (0, 1)
    ]
    return near, far


def started(sources, targets, arrived):
    copies = [
        pltpu.make_async_copy(source, target, arrived.at[i])
        for i, (source, target) in enumerate(zip(sources, targets))
    ]
    for copy in copies:
        copy.start()
    return copies


def attention_kernel(n_ctx, *refs):
    sources, (out_ref, own_ref), heads, targets, arrived = (
        refs[:6],
        refs[6:8],
        refs[8],
        refs[9:15],
        refs[15],
    )
    table, lengths, q_ref, k_ref, v_ref, residual_ref = targets
    copies = started(sources, targets, arrived)
    place = lax.axis_index("ctx")
    requests, slots, page_rows = q_ref.shape[0], k_ref.shape[1], k_ref.shape[2]
    span = table.shape[1]
    positions = slots * page_rows
    heads[...] = jnp.zeros_like(heads)
    for copy in copies[:3]:
        copy.wait()
    queries = q_ref[...].astype(F32)
    for r in range(requests):
        for h in range(HEADS):
            row = (h // GROUP) * ROWS + r * GROUP + h % GROUP
            heads[row : row + 1, :] = queries[r : r + 1, h * HEAD_DIM : (h + 1) * HEAD_DIM]
    at = lax.broadcasted_iota(jnp.int32, (ROWS, positions), 1)
    row_id = lax.broadcasted_iota(jnp.int32, (ROWS, positions), 0)
    slot, offset = at // page_rows, at % page_rows
    live = None
    for r in range(requests):
        seen = None
        for s in range(span):
            position = (s * n_ctx + place) * page_rows + offset
            here = (slot == table[r, s]) & (position < lengths[r])
            seen = here if seen is None else seen | here
        live = seen if live is None else jnp.where(row_id < r * GROUP, live.astype(jnp.int32), seen.astype(jnp.int32)) > 0
    out_row = lax.broadcasted_iota(jnp.int32, (ROWS, LANES), 0)
    diagonal = out_row == lax.broadcasted_iota(jnp.int32, (ROWS, LANES), 1)
    live = jnp.concatenate([live] * KV_HEADS, axis=0)
    copies[3].wait()
    keys = k_ref[0].reshape(positions, KV_HEADS * HEAD_DIM)
    query = heads[...].astype(BF16)

    def rows(k):
        return slice(k * ROWS, (k + 1) * ROWS)

    def lanes(k):
        return slice(k * HEAD_DIM, (k + 1) * HEAD_DIM)

    scores = jnp.concatenate(
        [
            lax.dot_general(
                query[rows(k)],
                keys[:, lanes(k)],
                (((1,), (1,)), ((), ())),
                preferred_element_type=F32,
            )
            for k in range(KV_HEADS)
        ],
        axis=0,
    )
    scores = jnp.where(live, scores * HEAD_DIM ** (-0.5), NEGATIVE)
    top = jnp.max(scores, axis=1, keepdims=True)
    weights = jnp.where(live, jnp.exp(scores - top), 0.0)
    total = jnp.sum(weights, axis=1, keepdims=True)
    high = weights.astype(BF16)
    low = (weights - high.astype(F32)).astype(BF16)
    used = requests * GROUP
    copies[4].wait()
    values = v_ref[0].reshape(positions, KV_HEADS * HEAD_DIM)
    for k in range(KV_HEADS):
        mixes = jnp.dot(
            jnp.concatenate([high[rows(k)], low[rows(k)]], axis=0),
            values[:, lanes(k)],
            preferred_element_type=F32,
        )
        mixes = mixes[:ROWS] + mixes[ROWS:]
        top_row = jnp.sum(jnp.where(diagonal, top[rows(k)], 0.0), axis=0, keepdims=True)
        total_row = jnp.sum(jnp.where(diagonal, total[rows(k)], 0.0), axis=0, keepdims=True)
        out_ref[k] = jnp.where(
            out_row < used, mixes, jnp.where(out_row == used, top_row, total_row)
        )
    copies[5].wait()
    width = own_ref.shape[1]
    own_ref[...] = residual_ref[:, pl.ds(pl.multiple_of(place * width, width), width)]


def attention_parts(queries, key_pages, value_pages, block_table, lengths, residual, n_ctx):
    vmem = pl.BlockSpec(memory_space=pltpu.VMEM)
    scalars, arrays = (block_table, lengths), (queries, key_pages, value_pages, residual)
    return pl.pallas_call(
        functools.partial(attention_kernel, n_ctx),
        out_shape=(
            pltpu.VMEM((KV_HEADS, ROWS, HEAD_DIM), F32),
            pltpu.VMEM((residual.shape[0], residual.shape[1] // n_ctx), BF16),
        ),
        in_specs=[pl.BlockSpec(memory_space=pltpu.HBM)] * 6,
        out_specs=(vmem, vmem),
        scratch_shapes=[pltpu.VMEM((KV_HEADS * ROWS, HEAD_DIM), F32)]
        + [pltpu.SMEM(x.shape, x.dtype) for x in scalars]
        + [pltpu.VMEM(x.shape, x.dtype) for x in arrays]
        + [pltpu.SemaphoreType.DMA((6,))],
        compiler_params=pltpu.CompilerParams(vmem_limit_bytes=KERNEL_VMEM),
        name="attention_parts",
    )(*(in_hbm(x) for x in scalars + arrays))


def merge_kernel(parts_ref, residual_ref, gain_ref, piece_ref, stream_ref, merged):
    n_src, kv_here = parts_ref.shape[0], parts_ref.shape[1]
    requests, width = stream_ref.shape
    used = requests * GROUP
    diagonal = lax.broadcasted_iota(jnp.int32, (ROWS, LANES), 0) == lax.broadcasted_iota(
        jnp.int32, (ROWS, LANES), 1
    )

    def column(row):
        return jnp.sum(jnp.where(diagonal, row, 0.0), axis=1, keepdims=True)

    for k in range(kv_here):
        tops = [column(parts_ref[s, k, used : used + 1, :]) for s in range(n_src)]
        totals = [column(parts_ref[s, k, used + 1 : used + 2, :]) for s in range(n_src)]
        top = functools.reduce(jnp.maximum, tops)
        scales = [jnp.exp(t - top) for t in tops]
        mixes = sum(parts_ref[s, k] * scales[s] for s in range(n_src))
        total = sum(totals[s] * scales[s] for s in range(n_src))
        mixes = mixes / total
        for r in range(requests):
            for g in range(GROUP):
                at = (k * GROUP + g) * HEAD_DIM
                merged[r : r + 1, at : at + HEAD_DIM] = mixes[r * GROUP + g : r * GROUP + g + 1, :]
    columns = pl.ds(pl.multiple_of(lax.axis_index("ctx") * width, width), width)
    stream = (residual_ref[...].astype(F32) + merged[...]).astype(BF16)
    stream_ref[...] = stream
    wide = stream.astype(F32)
    scaled = (wide * gain_ref[:, columns].astype(F32)).astype(BF16)
    square = jnp.sum(wide * wide, axis=1, keepdims=True)
    first = square.astype(BF16).astype(F32)
    second = (square - first).astype(BF16).astype(F32)
    third = square - first - second
    lane = lax.broadcasted_iota(jnp.int32, (requests, LANES), 1)
    spread = jnp.where(
        lane == 0, first, jnp.where(lane == 1, second, jnp.where(lane == 2, third, 0.0))
    )
    spread = spread.astype(BF16)
    for copy in range(piece_ref.shape[0]):
        piece_ref[copy, :, :width] = scaled
        piece_ref[copy, :, width:] = spread


def merge_parts(parts, residual, gain, width, copies):
    requests = residual.shape[0]
    vmem = pl.BlockSpec(memory_space=pltpu.VMEM)
    return pl.pallas_call(
        merge_kernel,
        out_shape=(
            pltpu.VMEM((copies, requests, width + LANES), BF16),
            jax.ShapeDtypeStruct((requests, width), BF16),
        ),
        in_specs=[vmem, vmem, vmem],
        out_specs=(vmem, vmem),
        scratch_shapes=[pltpu.VMEM((requests, width), F32)],
        compiler_params=pltpu.CompilerParams(vmem_limit_bytes=KERNEL_VMEM),
        name="merge_parts",
    )(in_vmem(parts), in_vmem(residual), gain)


def row_shares(table, blocks, core, n_req, rows):
    top, entries = table.shape[0] // 2, table.shape[1]
    per_exp = entries // (n_req * 2)
    requests = entries // per_exp // n_req
    half_z, half_y = n_req // 2, per_exp // 4
    row = lax.broadcasted_iota(jnp.int32, (entries, rows), 1)
    entry = lax.broadcasted_iota(jnp.int32, (entries, rows), 0)
    request, row = row % requests, row // requests
    yh, row = row % half_y, row // half_y
    zh, row = row % half_z, row // half_z
    yl, zl = row % 2, row // 2
    z = (2 * zh + zl + core) % n_req
    y = (2 * yh + yl + core) % (per_exp // 2)
    wanted = ((2 * y + core) * n_req + z) * requests + request
    pick = jnp.where(entry == wanted, 1.0, 0.0).astype(BF16)
    lines = []
    for block in blocks:
        named = table[:top] == block.astype(F32)
        line = jnp.sum(jnp.where(named, table[top:], 0.0), axis=0, keepdims=True)
        first = line.astype(BF16)
        second = (line - first.astype(F32)).astype(BF16)
        third = (line - first.astype(F32) - second.astype(F32)).astype(BF16)
        lines += [first, second, third]
    lines.append(jnp.zeros((16 - len(lines), entries), BF16))
    picked = jnp.dot(jnp.concatenate(lines, axis=0), pick, preferred_element_type=F32)
    return [picked[i : i + 1] + picked[i + 1 : i + 2] + picked[i + 2 : i + 3] for i in (0, 3)]


def expert_kernel(model_width, n_req, block_source, table_source, tokens_ref, *refs):
    sources, out_ref, held, block_expert, table_ref, turned, arrived = refs[:6], refs[6], refs[7:13], *refs[13:]
    sources, targets = (block_source, table_source) + sources, (block_expert, table_ref) + held
    copies = started(sources, targets, arrived)
    for copy in copies[:2]:
        copy.wait()
    copies = copies[2:]
    n_xl, quarters, n_xh, far_rows, width = out_ref.shape
    n_ctx, rows, hidden = n_xl * n_xh, quarters * far_rows, held[0].shape[1]
    contract = (((1,), (1,)), ((), ()))
    ones = jnp.ones((8, LANES), BF16)

    own = lax.axis_index("exp")
    core = lax.rem(own, 2)
    blocks = (block_expert[own], block_expert[own + 1 - 2 * core])
    shares = row_shares(table_ref[...], blocks, core, n_req, rows)

    def at(chunk):
        column = lax.rem(chunk + n_ctx - core, n_ctx)
        return column % n_xl, column // n_xl

    def added(total, term):
        return term if total is None else total + term

    squares = None
    for chunk in range(n_ctx):
        xl, xh = at(chunk)
        tokens = tokens_ref[xl, :, xh, :, width:].reshape(rows, LANES)
        squares = added(
            squares, lax.dot_general(ones, tokens, contract, preferred_element_type=F32)
        )
    scale = lax.rsqrt(squares[:1] / model_width + EPSILON)
    for chunk in range(n_ctx):
        xl, xh = at(chunk)
        tokens = tokens_ref[xl, :, xh, :, :width].reshape(rows, width)
        turned[chunk] = tokens.T
    active = []
    for b in range(2):
        for copy in copies[2 * b : 2 * b + 2]:
            copy.wait()
        products = None
        for chunk in range(n_ctx):
            columns = slice(chunk * width, (chunk + 1) * width)
            wide = jnp.concatenate([w[0, :, columns] for w in held[2 * b : 2 * b + 2]], axis=0)
            products = added(
                products, jnp.dot(wide, turned[chunk], preferred_element_type=F32)
            )
        gate, up = products[:hidden] * scale, products[hidden:] * scale
        active.append(gate / (1.0 + jnp.exp(-gate)) * up * shares[b])
    active.append(jnp.zeros((-2 * hidden % LANES, rows), F32))
    active = jnp.concatenate(active, axis=0).T[:, : 2 * hidden].astype(BF16)
    for copy in copies[4:]:
        copy.wait()
    for chunk in range(n_ctx):
        xl, xh = at(chunk)
        columns = slice(chunk * width, (chunk + 1) * width)
        down = jnp.concatenate([w[0, :, columns] for w in held[4:]], axis=0)
        total = jnp.dot(active, down, preferred_element_type=F32).astype(BF16)
        out_ref[xl, :, xh] = total.reshape(quarters, far_rows, width)


def routing_table(expert_routes, route_weights):
    top = expert_routes.shape[2]
    table = jnp.concatenate([expert_routes.astype(F32), route_weights], axis=2)
    return table.transpose(2, 0, 1).reshape(2 * top, -1)


def expert_partials(tokens, table, block_expert, weights, n_req):
    n_xl, quarters, n_xh, far_rows, padded = tokens.shape
    width = padded - LANES
    rows, model_width = quarters * far_rows, width * n_xl * n_xh
    hidden = weights[0].shape[1]
    hbm = pl.BlockSpec(memory_space=pltpu.HBM)
    vmem = pl.BlockSpec(memory_space=pltpu.VMEM)
    return pl.pallas_call(
        functools.partial(expert_kernel, float(model_width), n_req),
        out_shape=pltpu.VMEM((n_xl, quarters, n_xh, far_rows, width), BF16),
        in_specs=[hbm, hbm, vmem] + [hbm] * len(weights),
        out_specs=vmem,
        scratch_shapes=[pltpu.VMEM(w.shape, w.dtype) for w in weights]
        + [
            pltpu.SMEM(block_expert.shape, block_expert.dtype),
            pltpu.VMEM(table.shape, table.dtype),
            pltpu.VMEM((n_xl * n_xh, width, rows), BF16),
            pltpu.SemaphoreType.DMA((len(weights) + 2,)),
        ],
        compiler_params=pltpu.CompilerParams(vmem_limit_bytes=KERNEL_VMEM),
        cost_estimate=pl.CostEstimate(
            flops=12 * rows * hidden * model_width,
            bytes_accessed=12 * hidden * model_width,
            transcendentals=0,
        ),
        name="expert_partials",
    )(
        in_hbm(block_expert), in_hbm(table), in_vmem(tokens), *(in_hbm(w) for w in weights)
    )


def on_device(
    groups,
    queries,
    key_pages,
    value_pages,
    block_table,
    context_lengths,
    residual,
    norm_gain,
    gate_blocks,
    up_blocks,
    down_blocks,
    expert_routes,
    route_weights,
    block_expert,
):
    near, far = groups
    n_req, n_ctx, n_exp = (lax.axis_size(a) for a in AXES)
    requests, model_width = queries.shape
    width = model_width // n_ctx
    n_near, n_far = len(near[0]), len(far[0])
    far_rows = n_far // 2 * requests

    swap = [(i, i ^ 1) for i in range(n_exp)]
    gate_other, up_other, down_other = (
        lax.ppermute(w, "exp", swap) for w in (gate_blocks, up_blocks, down_blocks)
    )

    parts, residual = attention_parts(
        queries,
        key_pages,
        value_pages,
        block_table,
        context_lengths,
        residual,
        n_ctx,
    )
    parts = parts.reshape(n_ctx, KV_HEADS // n_ctx, ROWS, HEAD_DIM)
    parts = lax.all_to_all(parts, "ctx", 0, 0, tiled=True)
    piece, stream = merge_parts(
        parts, residual, norm_gain.reshape(1, model_width), width, n_far
    )

    def exchange(x, groups):
        return lax.all_to_all(x, AXES, 0, 0, axis_index_groups=groups, tiled=True)

    tokens = exchange(piece, far)
    tokens = tokens.reshape(2, far_rows, width + LANES)
    tokens = exchange(jnp.broadcast_to(tokens, (n_near,) + tokens.shape), near)
    tokens = tokens.reshape(2, n_near // 2, 2, far_rows, width + LANES)
    partials = expert_partials(
        tokens,
        routing_table(expert_routes, route_weights),
        block_expert,
        (gate_blocks, up_blocks, gate_other, up_other, down_blocks, down_other),
        n_req,
    )
    partials = exchange(partials.reshape(n_near, 2, far_rows, width), near)
    partials = jnp.sum(partials.astype(F32), axis=0).astype(BF16)
    partials = exchange(partials.reshape(n_far, requests, width), far)
    expert_sum = jnp.sum(partials.astype(F32), axis=0)
    return (stream.astype(F32) + expert_sum).astype(BF16)


def solution(mesh):
    in_specs = (
        P(("req", "exp"), None),
        P(("req", "exp"), "ctx", None, None),
        P(("req", "exp"), "ctx", None, None),
        P(("req", "exp"), "ctx"),
        P(("req", "exp")),
        P(("req", "exp"), None),
        P(),
        P("exp", ("req", "ctx"), None),
        P("exp", ("req", "ctx"), None),
        P("exp", ("req", "ctx"), None),
        P(),
        P(),
        P(),
    )
    out_specs = P(("req", "exp"), "ctx")
    groups = exchange_groups(*(mesh.shape[a] for a in AXES))
    return jax.shard_map(
        functools.partial(on_device, groups),
        mesh=mesh,
        in_specs=in_specs,
        out_specs=out_specs,
        check_vma=False,
    )
```

```python
import functools

import jax
import jax.numpy as jnp
import numpy as np
from jax import lax
from jax.experimental import pallas as pl
from jax.experimental.pallas import tpu as pltpu
from jax.sharding import PartitionSpec as P

HEADS = 48
KV_HEADS = 8
HEAD_DIM = 128
GROUP = HEADS // KV_HEADS
EPSILON = 1e-05
NEGATIVE = -1e30
ROWS = 16
LANES = 128
KERNEL_VMEM = 16 << 20
AXES = ("req", "ctx", "exp")
F32 = jnp.float32
BF16 = jnp.bfloat16


def in_vmem(x):
    return pltpu.with_memory_space_constraint(x, pltpu.VMEM)


def in_hbm(x):
    return pltpu.with_memory_space_constraint(x, pltpu.HBM)


def exchange_groups(n_req, n_ctx, n_exp):
    cols = n_exp // 2

    def device(z, x, y, core):
        z, x, y = (z + core) % n_req, (x + core) % n_ctx, (y + core) % cols
        return (z * n_ctx + x) * n_exp + y * 2 + core

    near = [
        [
            device(2 * zh + zl, 2 * xh + xl, 2 * yh + yl, core)
            for xl in (0, 1)
            for zl in (0, 1)
            for yl in (0, 1)
        ]
        for core in (0, 1)
        for xh in range(n_ctx // 2)
        for zh in range(n_req // 2)
        for yh in range(cols // 2)
    ]
    far = [
        [
            device(2 * zh + zl, 2 * xh + xl, 2 * yh + yl, core)
            for xh in range(n_ctx // 2)
            for zh in range(n_req // 2)
            for yh in range(cols // 2)
        ]
        for core in (0, 1)
        for xl in (0, 1)
        for zl in (0, 1)
        for yl in (0, 1)
    ]
    columns_far = [
        [
            device(2 * zh + zl, x, 2 * yh + yl, core)
            for zh in range(n_req // 2)
            for yh in range(cols // 2)
        ]
        for core in (0, 1)
        for x in range(n_ctx)
        for zl in (0, 1)
        for yl in (0, 1)
    ]
    return near, far, columns_far


def started(sources, targets, arrived):
    copies = [
        pltpu.make_async_copy(source, target, arrived.at[i])
        for i, (source, target) in enumerate(zip(sources, targets))
    ]
    for copy in copies:
        copy.start()
    return copies


def attention_kernel(n_ctx, *refs):
    sources, (out_ref, own_ref, scale_ref), heads, gains, targets, arrived = (
        refs[:7],
        refs[7:10],
        refs[10],
        refs[11],
        refs[12:19],
        refs[19],
    )
    table, lengths, q_ref, k_ref, v_ref, residual_ref, gain_ref = targets
    copies = started(sources, targets, arrived)
    place = lax.axis_index("ctx")
    requests, slots, page_rows = q_ref.shape[0], k_ref.shape[1], k_ref.shape[2]
    span = table.shape[1]
    positions = slots * page_rows
    heads[...] = jnp.zeros_like(heads)
    for copy in copies[:3]:
        copy.wait()
    queries = q_ref[...].astype(F32)
    for r in range(requests):
        for h in range(HEADS):
            row = (h // GROUP) * ROWS + r * GROUP + h % GROUP
            heads[row : row + 1, :] = queries[r : r + 1, h * HEAD_DIM : (h + 1) * HEAD_DIM]
    at = lax.broadcasted_iota(jnp.int32, (ROWS, positions), 1)
    row_id = lax.broadcasted_iota(jnp.int32, (ROWS, positions), 0)
    slot, offset = at // page_rows, at % page_rows
    live = None
    for r in range(requests):
        seen = None
        for s in range(span):
            position = (s * n_ctx + place) * page_rows + offset
            here = (slot == table[r, s]) & (position < lengths[r])
            seen = here if seen is None else seen | here
        live = seen if live is None else jnp.where(row_id < r * GROUP, live.astype(jnp.int32), seen.astype(jnp.int32)) > 0
    out_row = lax.broadcasted_iota(jnp.int32, (ROWS, LANES), 0)
    diagonal = out_row == lax.broadcasted_iota(jnp.int32, (ROWS, LANES), 1)
    live = jnp.concatenate([live] * KV_HEADS, axis=0)
    copies[3].wait()
    keys = k_ref[0].reshape(positions, KV_HEADS * HEAD_DIM)
    query = heads[...].astype(BF16)

    def rows(k):
        return slice(k * ROWS, (k + 1) * ROWS)

    def lanes(k):
        return slice(k * HEAD_DIM, (k + 1) * HEAD_DIM)

    scores = jnp.concatenate(
        [
            lax.dot_general(
                query[rows(k)],
                keys[:, lanes(k)],
                (((1,), (1,)), ((), ())),
                preferred_element_type=F32,
            )
            for k in range(KV_HEADS)
        ],
        axis=0,
    )
    scores = jnp.where(live, scores * HEAD_DIM ** (-0.5), NEGATIVE)
    top = jnp.max(scores, axis=1, keepdims=True)
    weights = jnp.where(live, jnp.exp(scores - top), 0.0)
    total = jnp.sum(weights, axis=1, keepdims=True)
    high = weights.astype(BF16)
    low = (weights - high.astype(F32)).astype(BF16)
    used = requests * GROUP
    copies[4].wait()
    values = v_ref[0].reshape(positions, KV_HEADS * HEAD_DIM)
    for k in range(KV_HEADS):
        mixes = jnp.dot(
            jnp.concatenate([high[rows(k)], low[rows(k)]], axis=0),
            values[:, lanes(k)],
            preferred_element_type=F32,
        )
        mixes = mixes[:ROWS] + mixes[ROWS:]
        top_row = jnp.sum(jnp.where(diagonal, top[rows(k)], 0.0), axis=0, keepdims=True)
        total_row = jnp.sum(jnp.where(diagonal, total[rows(k)], 0.0), axis=0, keepdims=True)
        part = jnp.where(
            out_row < used, mixes, jnp.where(out_row == used, top_row, total_row)
        )
        chunk, k = divmod(k, KV_HEADS // n_ctx)
        out_ref[chunk, 0, k] = part
        out_ref[(chunk + n_ctx // 2) % n_ctx, 1, k] = part
    for copy in copies[5:]:
        copy.wait()
    gains[...] = gain_ref[...].astype(F32)
    width = own_ref.shape[2]
    for i in range(2):
        column = lax.rem(place + i * (n_ctx // 2), n_ctx)
        own_ref[i] = residual_ref[:, pl.ds(pl.multiple_of(column * width, width), width)]
        for h in range(width // LANES):
            row = gains[pl.ds(column * (width // LANES) + h, 1), :]
            scale_ref[i, :, h * LANES : (h + 1) * LANES] = row


def attention_parts(
    queries, key_pages, value_pages, block_table, lengths, residual, gain, n_ctx
):
    vmem = pl.BlockSpec(memory_space=pltpu.VMEM)
    scalars, arrays = (block_table, lengths), (queries, key_pages, value_pages, residual, gain)
    return pl.pallas_call(
        functools.partial(attention_kernel, n_ctx),
        out_shape=(
            pltpu.VMEM((n_ctx, 2, KV_HEADS // n_ctx, ROWS, HEAD_DIM), F32),
            pltpu.VMEM((2, residual.shape[0], residual.shape[1] // n_ctx), BF16),
            pltpu.VMEM((2, 1, residual.shape[1] // n_ctx), F32),
        ),
        in_specs=[pl.BlockSpec(memory_space=pltpu.HBM)] * 7,
        out_specs=(vmem, vmem, vmem),
        scratch_shapes=[pltpu.VMEM((KV_HEADS * ROWS, HEAD_DIM), F32), pltpu.VMEM(gain.shape, F32)]
        + [pltpu.SMEM(x.shape, x.dtype) for x in scalars]
        + [pltpu.VMEM(x.shape, x.dtype) for x in arrays]
        + [pltpu.SemaphoreType.DMA((7,))],
        compiler_params=pltpu.CompilerParams(vmem_limit_bytes=KERNEL_VMEM),
        name="attention_parts",
    )(*(in_hbm(x) for x in scalars + arrays))


def merge_kernel(parts_ref, residual_ref, gain_ref, piece_ref, stream_ref, merged):
    n_src, kv_here = parts_ref.shape[0], parts_ref.shape[2]
    requests, width = stream_ref.shape
    used = requests * GROUP
    place = lax.axis_index("ctx")
    core = lax.rem(lax.axis_index("exp"), 2)
    diagonal = lax.broadcasted_iota(jnp.int32, (ROWS, LANES), 0) == lax.broadcasted_iota(
        jnp.int32, (ROWS, LANES), 1
    )

    def column(row):
        return jnp.sum(jnp.where(diagonal, row, 0.0), axis=1, keepdims=True)

    scaled, square = [], 0.0
    for i in range(2):
        for k in range(kv_here):
            tops = [column(parts_ref[s, i, k, used : used + 1, :]) for s in range(n_src)]
            totals = [column(parts_ref[s, i, k, used + 1 : used + 2, :]) for s in range(n_src)]
            top = functools.reduce(jnp.maximum, tops)
            scales = [jnp.exp(t - top) for t in tops]
            mixes = sum(parts_ref[s, i, k] * scales[s] for s in range(n_src))
            total = sum(totals[s] * scales[s] for s in range(n_src))
            mixes = mixes / total
            for r in range(requests):
                for g in range(GROUP):
                    at = (k * GROUP + g) * HEAD_DIM
                    row = r * GROUP + g
                    merged[i, r : r + 1, at : at + HEAD_DIM] = mixes[row : row + 1, :]
        stream = (residual_ref[i].astype(F32) + merged[i]).astype(BF16)
        if i == 0:
            stream_ref[...] = stream
        wide = stream.astype(F32)
        scaled.append(wide * gain_ref[i])
        square += jnp.sum(wide * wide, axis=1, keepdims=True)
    first = square.astype(BF16).astype(F32)
    second = (square - first).astype(BF16).astype(F32)
    third = square - first - second
    lane = lax.broadcasted_iota(jnp.int32, (requests, LANES), 1)
    spread = jnp.where(
        lane == 0, first, jnp.where(lane == 1, second, jnp.where(lane == 2, third, 0.0))
    ).astype(BF16)
    upper = lax.rem(place - core + n_src, n_src) >= n_src // 2
    low = jnp.where(upper, scaled[1], scaled[0]).astype(BF16)
    high = jnp.where(upper, scaled[0], scaled[1]).astype(BF16)
    for copy in range(piece_ref.shape[0]):
        piece_ref[copy, :, :width] = low
        piece_ref[copy, :, width : 2 * width] = high
        piece_ref[copy, :, 2 * width :] = spread


def merge_parts(parts, residual, gain, copies):
    _, requests, width = residual.shape
    vmem = pl.BlockSpec(memory_space=pltpu.VMEM)
    return pl.pallas_call(
        merge_kernel,
        out_shape=(
            pltpu.VMEM((copies, requests, 2 * width + LANES), BF16),
            jax.ShapeDtypeStruct((requests, width), BF16),
        ),
        in_specs=[vmem, vmem, vmem],
        out_specs=(vmem, vmem),
        scratch_shapes=[pltpu.VMEM((2, requests, width), F32)],
        compiler_params=pltpu.CompilerParams(vmem_limit_bytes=KERNEL_VMEM),
        name="merge_parts",
    )(in_vmem(parts), in_vmem(residual), in_vmem(gain))


def row_shares(routes_ref, weights_ref, blocks, core, requests, rows):
    n_exp, _, entries = routes_ref.shape
    n_req, half_y = entries // requests, n_exp // 4
    row = lax.broadcasted_iota(jnp.int32, (entries, rows), 1)
    entry = lax.broadcasted_iota(jnp.int32, (entries, rows), 0)
    request, row = row % requests, row // requests
    yh, row = row % half_y, row // half_y
    zh, row = row % (n_req // 2), row // (n_req // 2)
    yl, zl = row % 2, row // 2
    here = entry == (2 * zh + zl + core) % n_req * requests + request
    y = (2 * yh + yl + core) % (n_exp // 2)
    diagonal = lax.broadcasted_iota(jnp.int32, (entries, entries), 0) == lax.broadcasted_iota(
        jnp.int32, (entries, entries), 1
    )
    shares = [jnp.zeros((entries, rows), F32) for _ in blocks]
    for column in range(n_exp // 2):
        routes, weights = routes_ref[2 * column + core], weights_ref[2 * column + core]
        at = here & (y == column)
        for b, block in enumerate(blocks):
            line = jnp.sum(jnp.where(routes == block, weights, 0.0), axis=0, keepdims=True)
            upright = jnp.sum(jnp.where(diagonal, line, 0.0), axis=1, keepdims=True)
            shares[b] += jnp.where(at, upright, 0.0)
    return [jnp.sum(share, axis=0, keepdims=True) for share in shares]


def expert_kernel(model_width, requests, block_source, route_source, weight_source, tokens_ref, *refs):
    sources, gate_held, out_ref, held = refs[:5], refs[5], refs[6], refs[7:12]
    block_expert, routes_ref, weights_ref, turned, arrived = refs[12:]
    copies = started(
        (block_source, route_source, weight_source) + sources,
        (block_expert, routes_ref, weights_ref) + held,
        arrived,
    )
    held = (gate_held,) + held
    for copy in copies[:3]:
        copy.wait()
    copies = copies[3:]
    n_xl, quarters, n_xh, far_rows, width = out_ref.shape
    n_ctx, rows, hidden = n_xl * n_xh, quarters * far_rows, held[0].shape[1]
    contract = (((1,), (1,)), ((), ()))
    ones = jnp.ones((8, LANES), BF16)

    own = lax.axis_index("exp")
    core = lax.rem(own, 2)
    blocks = (block_expert[own + 1 - 2 * core], block_expert[own])
    shares = row_shares(routes_ref, weights_ref, blocks, core, requests, rows)

    def at(chunk):
        column = lax.rem(chunk + n_ctx - core, n_ctx)
        return column % n_xl, column // n_xl

    def added(total, term):
        return term if total is None else total + term

    squares = None
    for xl in range(n_xl):
        tokens = tokens_ref[xl, :, :, n_xh * width :].reshape(rows, LANES)
        squares = added(
            squares, lax.dot_general(ones, tokens, contract, preferred_element_type=F32)
        )
        for xh in range(n_xh):
            tokens = tokens_ref[xl, :, :, xh * width : (xh + 1) * width].reshape(rows, width)
            turned[lax.rem(xh * n_xl + xl + core, n_ctx)] = tokens.T
    scale = lax.rsqrt(squares[:1] / model_width + EPSILON)
    active = []
    for b in range(2):
        for copy in copies[1:3] if b else copies[:1]:
            copy.wait()
        products = None
        for chunk in range(n_ctx):
            columns = slice(chunk * width, (chunk + 1) * width)
            wide = jnp.concatenate([w[0, :, columns] for w in held[2 * b : 2 * b + 2]], axis=0)
            products = added(
                products, jnp.dot(wide, turned[chunk], preferred_element_type=F32)
            )
        gate, up = products[:hidden] * scale, products[hidden:] * scale
        active.append(gate / (1.0 + jnp.exp(-gate)) * up * shares[b])
    active.append(jnp.zeros((-2 * hidden % LANES, rows), F32))
    active = jnp.concatenate(active, axis=0).T[:, : 2 * hidden].astype(BF16)
    for copy in copies[3:]:
        copy.wait()
    for chunk in range(n_ctx):
        xl, xh = at(chunk)
        columns = slice(chunk * width, (chunk + 1) * width)
        down = jnp.concatenate([w[0, :, columns] for w in held[4:]], axis=0)
        total = jnp.dot(active, down, preferred_element_type=F32).astype(BF16)
        out_ref[xl, :, xh] = total.reshape(quarters, far_rows, width)


def expert_partials(
    tokens, routes, route_weights, block_expert, gate_other, weights, requests
):
    n_xl, quarters, far_rows, padded = tokens.shape
    n_xh = 2
    width = (padded - LANES) // n_xh
    rows, model_width = quarters * far_rows, width * n_xl * n_xh
    hidden = weights[0].shape[1]
    hbm = pl.BlockSpec(memory_space=pltpu.HBM)
    vmem = pl.BlockSpec(memory_space=pltpu.VMEM)
    return pl.pallas_call(
        functools.partial(expert_kernel, float(model_width), requests),
        out_shape=pltpu.VMEM((n_xl, quarters, n_xh, far_rows, width), BF16),
        in_specs=[hbm, hbm, hbm, vmem] + [hbm] * len(weights) + [vmem],
        out_specs=vmem,
        scratch_shapes=[pltpu.VMEM(w.shape, w.dtype) for w in weights]
        + [
            pltpu.SMEM(block_expert.shape, block_expert.dtype),
            pltpu.VMEM(routes.shape, routes.dtype),
            pltpu.VMEM(route_weights.shape, route_weights.dtype),
            pltpu.VMEM((n_xl * n_xh, width, rows), BF16),
            pltpu.SemaphoreType.DMA((len(weights) + 3,)),
        ],
        compiler_params=pltpu.CompilerParams(vmem_limit_bytes=KERNEL_VMEM),
        cost_estimate=pl.CostEstimate(
            flops=12 * rows * hidden * model_width,
            bytes_accessed=12 * hidden * model_width,
            transcendentals=0,
        ),
        name="expert_partials",
    )(
        *(in_hbm(x) for x in (block_expert, routes, route_weights)),
        in_vmem(tokens),
        *(in_hbm(w) for w in weights),
        in_vmem(gate_other),
    )


def on_device(
    groups,
    queries,
    key_pages,
    value_pages,
    block_table,
    context_lengths,
    residual,
    norm_gain,
    gate_blocks,
    up_blocks,
    down_blocks,
    expert_routes,
    route_weights,
    block_expert,
):
    near, far, columns_far = groups
    n_req, n_ctx, n_exp = (lax.axis_size(a) for a in AXES)
    requests, model_width = queries.shape
    width = model_width // n_ctx
    n_near, n_far = len(near[0]), len(far[0])
    far_rows = len(columns_far[0]) * requests

    swap = [(i, i ^ 1) for i in range(n_exp)]
    gate_other, up_other, down_other = (
        lax.ppermute(w, "exp", swap) for w in (gate_blocks, up_blocks, down_blocks)
    )

    parts, residual, gain = attention_parts(
        queries,
        key_pages,
        value_pages,
        block_table,
        context_lengths,
        residual,
        norm_gain.reshape(-1, LANES),
        n_ctx,
    )
    parts = lax.all_to_all(parts, "ctx", 0, 0, tiled=True)
    piece, stream = merge_parts(parts, residual, gain, len(columns_far[0]))

    def exchange(x, groups):
        return lax.all_to_all(x, AXES, 0, 0, axis_index_groups=groups, tiled=True)

    tokens = exchange(piece, columns_far)
    tokens = tokens.reshape(far_rows, piece.shape[2])
    tokens = exchange(jnp.broadcast_to(tokens, (n_near,) + tokens.shape), near)
    tokens = tokens.reshape(2, n_near // 2, far_rows, piece.shape[2])
    partials = expert_partials(
        tokens,
        expert_routes.transpose(0, 2, 1),
        route_weights.transpose(0, 2, 1),
        block_expert,
        gate_other,
        (up_other, gate_blocks, up_blocks, down_other, down_blocks),
        requests,
    )
    partials = exchange(partials.reshape(n_near, 2, far_rows, width), near)
    partials = jnp.sum(partials.astype(F32), axis=0).astype(BF16)
    partials = exchange(partials.reshape(n_far, requests, width), far)
    expert_sum = jnp.sum(partials.astype(F32), axis=0)
    return (stream.astype(F32) + expert_sum).astype(BF16)


def solution(mesh):
    in_specs = (
        P(("req", "exp"), None),
        P(("req", "exp"), "ctx", None, None),
        P(("req", "exp"), "ctx", None, None),
        P(("req", "exp"), "ctx"),
        P(("req", "exp")),
        P(("req", "exp"), None),
        P(),
        P("exp", ("req", "ctx"), None),
        P("exp", ("req", "ctx"), None),
        P("exp", ("req", "ctx"), None),
        P(),
        P(),
        P(),
    )
    out_specs = P(("req", "exp"), "ctx")
    groups = exchange_groups(*(mesh.shape[a] for a in AXES))
    return jax.shard_map(
        functools.partial(on_device, groups),
        mesh=mesh,
        in_specs=in_specs,
        out_specs=out_specs,
        check_vma=False,
    )
```

```python
import functools

import jax
import jax.numpy as jnp
import numpy as np
from jax import lax
from jax.experimental import pallas as pl
from jax.experimental.pallas import tpu as pltpu
from jax.sharding import PartitionSpec as P

HEADS = 48
KV_HEADS = 8
HEAD_DIM = 128
GROUP = HEADS // KV_HEADS
EPSILON = 1e-05
NEGATIVE = -1e30
ROWS = 16
LANES = 128
KERNEL_VMEM = 16 << 20
AXES = ("req", "ctx", "exp")
QUARTERS = ((0, 0), (1, 0), (1, 1), (0, 1))
F32 = jnp.float32
BF16 = jnp.bfloat16


def in_vmem(x):
    return pltpu.with_memory_space_constraint(x, pltpu.VMEM)


def in_hbm(x):
    return pltpu.with_memory_space_constraint(x, pltpu.HBM)


def exchange_groups(n_req, n_ctx, n_exp):
    cols = n_exp // 2

    def device(z, x, y, core):
        z, x, y = (z + core) % n_req, (x + core) % n_ctx, (y + core) % cols
        return (z * n_ctx + x) * n_exp + y * 2 + core

    near = [
        [
            device(2 * zh + zl, 2 * xh + xl, 2 * yh + yl, core)
            for quarter, (zl, yl) in enumerate(QUARTERS)
            for xl in (quarter % 2, 1 - quarter % 2)
        ]
        for core in (0, 1)
        for xh in range(n_ctx // 2)
        for zh in range(n_req // 2)
        for yh in range(cols // 2)
    ]
    far = [
        [
            device(2 * zh + zl, 2 * xh + xl, 2 * yh + yl, core)
            for yh in range(cols // 2)
            for zh in range(n_req // 2)
            for xh in range(n_ctx // 2)
        ]
        for core in (0, 1)
        for xl in (0, 1)
        for zl in (0, 1)
        for yl in (0, 1)
    ]
    columns_far = [
        [
            device(2 * zh + zl, x, 2 * yh + yl, core)
            for zh in range(n_req // 2)
            for yh in range(cols // 2)
        ]
        for core in (0, 1)
        for x in range(n_ctx)
        for zl in (0, 1)
        for yl in (0, 1)
    ]
    return near, far, columns_far


def started(sources, targets, arrived):
    copies = [
        pltpu.make_async_copy(source, target, arrived.at[i])
        for i, (source, target) in enumerate(zip(sources, targets))
    ]
    for copy in copies:
        copy.start()
    return copies


def attention_kernel(n_ctx, *refs):
    sources, (out_ref, own_ref, scale_ref), heads, gains, targets, arrived = (
        refs[:7],
        refs[7:10],
        refs[10],
        refs[11],
        refs[12:19],
        refs[19],
    )
    table, lengths, q_ref, k_ref, v_ref, residual_ref, gain_ref = targets
    copies = started(sources, targets, arrived)
    place = lax.axis_index("ctx")
    requests, slots, page_rows = q_ref.shape[0], k_ref.shape[1], k_ref.shape[2]
    span = table.shape[1]
    positions = slots * page_rows
    heads[...] = jnp.zeros_like(heads)
    for copy in copies[:3]:
        copy.wait()
    queries = q_ref[...].astype(F32)
    for r in range(requests):
        for h in range(HEADS):
            row = (h // GROUP) * ROWS + r * GROUP + h % GROUP
            heads[row : row + 1, :] = queries[r : r + 1, h * HEAD_DIM : (h + 1) * HEAD_DIM]
    at = lax.broadcasted_iota(jnp.int32, (ROWS, positions), 1)
    row_id = lax.broadcasted_iota(jnp.int32, (ROWS, positions), 0)
    slot, offset = at // page_rows, at % page_rows
    live = None
    for r in range(requests):
        seen = None
        for s in range(span):
            position = (s * n_ctx + place) * page_rows + offset
            here = (slot == table[r, s]) & (position < lengths[r])
            seen = here if seen is None else seen | here
        live = seen if live is None else jnp.where(row_id < r * GROUP, live.astype(jnp.int32), seen.astype(jnp.int32)) > 0
    out_row = lax.broadcasted_iota(jnp.int32, (ROWS, LANES), 0)
    diagonal = out_row == lax.broadcasted_iota(jnp.int32, (ROWS, LANES), 1)
    live = jnp.concatenate([live] * KV_HEADS, axis=0)
    copies[3].wait()
    keys = k_ref[0].reshape(positions, KV_HEADS * HEAD_DIM)
    query = heads[...].astype(BF16)

    def rows(k):
        return slice(k * ROWS, (k + 1) * ROWS)

    def lanes(k):
        return slice(k * HEAD_DIM, (k + 1) * HEAD_DIM)

    scores = jnp.concatenate(
        [
            lax.dot_general(
                query[rows(k)],
                keys[:, lanes(k)],
                (((1,), (1,)), ((), ())),
                preferred_element_type=F32,
            )
            for k in range(KV_HEADS)
        ],
        axis=0,
    )
    scores = jnp.where(live, scores * HEAD_DIM ** (-0.5), NEGATIVE)
    top = jnp.max(scores, axis=1, keepdims=True)
    weights = jnp.where(live, jnp.exp(scores - top), 0.0)
    total = jnp.sum(weights, axis=1, keepdims=True)
    high = weights.astype(BF16)
    low = (weights - high.astype(F32)).astype(BF16)
    used = requests * GROUP
    copies[4].wait()
    values = v_ref[0].reshape(positions, KV_HEADS * HEAD_DIM)
    for k in range(KV_HEADS):
        mixes = jnp.dot(
            jnp.concatenate([high[rows(k)], low[rows(k)]], axis=0),
            values[:, lanes(k)],
            preferred_element_type=F32,
        )
        mixes = mixes[:ROWS] + mixes[ROWS:]
        top_row = jnp.sum(jnp.where(diagonal, top[rows(k)], 0.0), axis=0, keepdims=True)
        total_row = jnp.sum(jnp.where(diagonal, total[rows(k)], 0.0), axis=0, keepdims=True)
        part = jnp.where(
            out_row < used, mixes, jnp.where(out_row == used, top_row, total_row)
        )
        chunk, k = divmod(k, KV_HEADS // n_ctx)
        out_ref[chunk, 0, k] = part
        out_ref[(chunk + n_ctx // 2) % n_ctx, 1, k] = part
    for copy in copies[5:]:
        copy.wait()
    gains[...] = gain_ref[...].astype(F32)
    width = own_ref.shape[2]
    for i in range(2):
        column = lax.rem(place + i * (n_ctx // 2), n_ctx)
        own_ref[i] = residual_ref[:, pl.ds(pl.multiple_of(column * width, width), width)]
        for h in range(width // LANES):
            row = gains[pl.ds(column * (width // LANES) + h, 1), :]
            scale_ref[i, :, h * LANES : (h + 1) * LANES] = row


def attention_parts(
    queries, key_pages, value_pages, block_table, lengths, residual, gain, n_ctx
):
    vmem = pl.BlockSpec(memory_space=pltpu.VMEM)
    scalars, arrays = (block_table, lengths), (queries, key_pages, value_pages, residual, gain)
    return pl.pallas_call(
        functools.partial(attention_kernel, n_ctx),
        out_shape=(
            pltpu.VMEM((n_ctx, 2, KV_HEADS // n_ctx, ROWS, HEAD_DIM), F32),
            pltpu.VMEM((2, residual.shape[0], residual.shape[1] // n_ctx), BF16),
            pltpu.VMEM((2, 1, residual.shape[1] // n_ctx), F32),
        ),
        in_specs=[pl.BlockSpec(memory_space=pltpu.HBM)] * 7,
        out_specs=(vmem, vmem, vmem),
        scratch_shapes=[pltpu.VMEM((KV_HEADS * ROWS, HEAD_DIM), F32), pltpu.VMEM(gain.shape, F32)]
        + [pltpu.SMEM(x.shape, x.dtype) for x in scalars]
        + [pltpu.VMEM(x.shape, x.dtype) for x in arrays]
        + [pltpu.SemaphoreType.DMA((7,))],
        compiler_params=pltpu.CompilerParams(vmem_limit_bytes=KERNEL_VMEM),
        name="attention_parts",
    )(*(in_hbm(x) for x in scalars + arrays))


def merge_kernel(parts_ref, residual_ref, gain_ref, piece_ref, stream_ref, merged):
    n_src, kv_here = parts_ref.shape[0], parts_ref.shape[2]
    requests, width = stream_ref.shape
    used = requests * GROUP
    place = lax.axis_index("ctx")
    core = lax.rem(lax.axis_index("exp"), 2)
    diagonal = lax.broadcasted_iota(jnp.int32, (ROWS, LANES), 0) == lax.broadcasted_iota(
        jnp.int32, (ROWS, LANES), 1
    )

    def column(row):
        return jnp.sum(jnp.where(diagonal, row, 0.0), axis=1, keepdims=True)

    scaled, square = [], 0.0
    for i in range(2):
        for k in range(kv_here):
            tops = [column(parts_ref[s, i, k, used : used + 1, :]) for s in range(n_src)]
            totals = [column(parts_ref[s, i, k, used + 1 : used + 2, :]) for s in range(n_src)]
            top = functools.reduce(jnp.maximum, tops)
            scales = [jnp.exp(t - top) for t in tops]
            mixes = sum(parts_ref[s, i, k] * scales[s] for s in range(n_src))
            total = sum(totals[s] * scales[s] for s in range(n_src))
            mixes = mixes / total
            for r in range(requests):
                for g in range(GROUP):
                    at = (k * GROUP + g) * HEAD_DIM
                    row = r * GROUP + g
                    merged[i, r : r + 1, at : at + HEAD_DIM] = mixes[row : row + 1, :]
        stream = (residual_ref[i].astype(F32) + merged[i]).astype(BF16)
        if i == 0:
            stream_ref[...] = stream
        wide = stream.astype(F32)
        scaled.append(wide * gain_ref[i])
        square += jnp.sum(wide * wide, axis=1, keepdims=True)
    first = square.astype(BF16).astype(F32)
    second = (square - first).astype(BF16).astype(F32)
    third = square - first - second
    lane = lax.broadcasted_iota(jnp.int32, (requests, LANES), 1)
    spread = jnp.where(
        lane == 0, first, jnp.where(lane == 1, second, jnp.where(lane == 2, third, 0.0))
    ).astype(BF16)
    upper = lax.rem(place - core + n_src, n_src) >= n_src // 2
    low = jnp.where(upper, scaled[1], scaled[0]).astype(BF16)
    high = jnp.where(upper, scaled[0], scaled[1]).astype(BF16)
    for copy in range(piece_ref.shape[0]):
        piece_ref[copy, :, :width] = low
        piece_ref[copy, :, width : 2 * width] = high
        piece_ref[copy, :, 2 * width :] = spread


def merge_parts(parts, residual, gain, copies):
    _, requests, width = residual.shape
    vmem = pl.BlockSpec(memory_space=pltpu.VMEM)
    return pl.pallas_call(
        merge_kernel,
        out_shape=(
            pltpu.VMEM((copies, requests, 2 * width + LANES), BF16),
            jax.ShapeDtypeStruct((requests, width), BF16),
        ),
        in_specs=[vmem, vmem, vmem],
        out_specs=(vmem, vmem),
        scratch_shapes=[pltpu.VMEM((2, requests, width), F32)],
        compiler_params=pltpu.CompilerParams(vmem_limit_bytes=KERNEL_VMEM),
        name="merge_parts",
    )(in_vmem(parts), in_vmem(residual), in_vmem(gain))


def row_shares(routes_ref, weights_ref, blocks, core, requests, rows):
    n_exp, _, entries = routes_ref.shape
    n_req, half_y = entries // requests, n_exp // 4
    row = lax.broadcasted_iota(jnp.int32, (entries, rows), 1)
    entry = lax.broadcasted_iota(jnp.int32, (entries, rows), 0)
    request, row = row % requests, row // requests
    yh, row = row % half_y, row // half_y
    zh, row = row % (n_req // 2), row // (n_req // 2)
    zl = sum((row == q).astype(jnp.int32) * QUARTERS[q][0] for q in range(4))
    yl = sum((row == q).astype(jnp.int32) * QUARTERS[q][1] for q in range(4))
    here = entry == (2 * zh + zl + core) % n_req * requests + request
    y = (2 * yh + yl + core) % (n_exp // 2)
    diagonal = lax.broadcasted_iota(jnp.int32, (entries, entries), 0) == lax.broadcasted_iota(
        jnp.int32, (entries, entries), 1
    )
    shares = [jnp.zeros((entries, rows), F32) for _ in blocks]
    for column in range(n_exp // 2):
        routes, weights = routes_ref[2 * column + core], weights_ref[2 * column + core]
        at = here & (y == column)
        for b, block in enumerate(blocks):
            line = jnp.sum(jnp.where(routes == block, weights, 0.0), axis=0, keepdims=True)
            upright = jnp.sum(jnp.where(diagonal, line, 0.0), axis=1, keepdims=True)
            shares[b] += jnp.where(at, upright, 0.0)
    return [jnp.sum(share, axis=0, keepdims=True) for share in shares]


def expert_kernel(model_width, requests, block_source, route_source, weight_source, tokens_ref, *refs):
    sources, gate_held, out_ref, held = refs[:5], refs[5], refs[6], refs[7:12]
    block_expert, routes_ref, weights_ref, turned, arrived = refs[12:]
    copies = started(
        (block_source, route_source, weight_source) + sources,
        (block_expert, routes_ref, weights_ref) + held,
        arrived,
    )
    held = (gate_held,) + held
    for copy in copies[:3]:
        copy.wait()
    copies = copies[3:]
    quarters, n_xl, n_xh, far_rows, width = out_ref.shape
    n_ctx, rows, hidden = n_xl * n_xh, quarters * far_rows, held[0].shape[1]
    contract = (((1,), (1,)), ((), ()))
    ones = jnp.ones((8, LANES), BF16)

    own = lax.axis_index("exp")
    core = lax.rem(own, 2)
    blocks = (block_expert[own + 1 - 2 * core], block_expert[own])
    shares = row_shares(routes_ref, weights_ref, blocks, core, requests, rows)

    def at(chunk):
        column = lax.rem(chunk + n_ctx - core, n_ctx)
        return column % n_xl, column // n_xl

    def own_rows(xl, columns):
        return jnp.concatenate(
            [tokens_ref[q, (xl + q) % n_xl, :, columns] for q in range(quarters)], axis=0
        )

    def added(total, term):
        return term if total is None else total + term

    squares = None
    for xl in range(n_xl):
        tokens = own_rows(xl, slice(n_xh * width, n_xh * width + LANES))
        squares = added(
            squares, lax.dot_general(ones, tokens, contract, preferred_element_type=F32)
        )
        for xh in range(n_xh):
            tokens = own_rows(xl, slice(xh * width, (xh + 1) * width))
            turned[lax.rem(xh * n_xl + xl + core, n_ctx)] = tokens.T
    scale = lax.rsqrt(squares[:1] / model_width + EPSILON)
    active = []
    for b in range(2):
        for copy in copies[1:3] if b else copies[:1]:
            copy.wait()
        products = None
        for chunk in range(n_ctx):
            columns = slice(chunk * width, (chunk + 1) * width)
            wide = jnp.concatenate([w[0, :, columns] for w in held[2 * b : 2 * b + 2]], axis=0)
            products = added(
                products, jnp.dot(wide, turned[chunk], preferred_element_type=F32)
            )
        gate, up = products[:hidden] * scale, products[hidden:] * scale
        active.append(gate / (1.0 + jnp.exp(-gate)) * up * shares[b])
    active.append(jnp.zeros((-2 * hidden % LANES, rows), F32))
    active = jnp.concatenate(active, axis=0).T[:, : 2 * hidden].astype(BF16)
    for copy in copies[3:]:
        copy.wait()
    for chunk in range(n_ctx):
        xl, xh = at(chunk)
        columns = slice(chunk * width, (chunk + 1) * width)
        down = jnp.concatenate([w[0, :, columns] for w in held[4:]], axis=0)
        total = jnp.dot(active, down, preferred_element_type=F32).astype(BF16)
        for q in range(quarters):
            out_ref[q, lax.rem(xl + q, n_xl), xh] = total[q * far_rows : (q + 1) * far_rows]


def expert_partials(
    tokens, routes, route_weights, block_expert, gate_other, weights, requests
):
    quarters, n_xl, far_rows, padded = tokens.shape
    n_xh = 2
    width = (padded - LANES) // n_xh
    rows, model_width = quarters * far_rows, width * n_xl * n_xh
    hidden = weights[0].shape[1]
    hbm = pl.BlockSpec(memory_space=pltpu.HBM)
    vmem = pl.BlockSpec(memory_space=pltpu.VMEM)
    return pl.pallas_call(
        functools.partial(expert_kernel, float(model_width), requests),
        out_shape=pltpu.VMEM((quarters, n_xl, n_xh, far_rows, width), BF16),
        in_specs=[hbm, hbm, hbm, vmem] + [hbm] * len(weights) + [vmem],
        out_specs=vmem,
        scratch_shapes=[pltpu.VMEM(w.shape, w.dtype) for w in weights]
        + [
            pltpu.SMEM(block_expert.shape, block_expert.dtype),
            pltpu.VMEM(routes.shape, routes.dtype),
            pltpu.VMEM(route_weights.shape, route_weights.dtype),
            pltpu.VMEM((n_xl * n_xh, width, rows), BF16),
            pltpu.SemaphoreType.DMA((len(weights) + 3,)),
        ],
        compiler_params=pltpu.CompilerParams(vmem_limit_bytes=KERNEL_VMEM),
        cost_estimate=pl.CostEstimate(
            flops=12 * rows * hidden * model_width,
            bytes_accessed=12 * hidden * model_width,
            transcendentals=0,
        ),
        name="expert_partials",
    )(
        *(in_hbm(x) for x in (block_expert, routes, route_weights)),
        in_vmem(tokens),
        *(in_hbm(w) for w in weights),
        in_vmem(gate_other),
    )


def on_device(
    groups,
    queries,
    key_pages,
    value_pages,
    block_table,
    context_lengths,
    residual,
    norm_gain,
    gate_blocks,
    up_blocks,
    down_blocks,
    expert_routes,
    route_weights,
    block_expert,
):
    near, far, columns_far = groups
    n_req, n_ctx, n_exp = (lax.axis_size(a) for a in AXES)
    requests, model_width = queries.shape
    width = model_width // n_ctx
    n_near, n_far = len(near[0]), len(far[0])
    far_rows = len(columns_far[0]) * requests

    swap = [(i, i ^ 1) for i in range(n_exp)]
    gate_other, up_other, down_other = (
        lax.ppermute(w, "exp", swap) for w in (gate_blocks, up_blocks, down_blocks)
    )

    parts, residual, gain = attention_parts(
        queries,
        key_pages,
        value_pages,
        block_table,
        context_lengths,
        residual,
        norm_gain.reshape(-1, LANES),
        n_ctx,
    )
    parts = lax.all_to_all(parts, "ctx", 0, 0, tiled=True)
    piece, stream = merge_parts(parts, residual, gain, len(columns_far[0]))

    def exchange(x, groups):
        return lax.all_to_all(x, AXES, 0, 0, axis_index_groups=groups, tiled=True)

    tokens = exchange(piece, columns_far)
    tokens = tokens.reshape(far_rows, piece.shape[2])
    tokens = exchange(jnp.broadcast_to(tokens, (n_near,) + tokens.shape), near)
    tokens = tokens.reshape(n_near // 2, 2, far_rows, piece.shape[2])
    partials = expert_partials(
        tokens,
        expert_routes.transpose(0, 2, 1),
        route_weights.transpose(0, 2, 1),
        block_expert,
        gate_other,
        (up_other, gate_blocks, up_blocks, down_other, down_blocks),
        requests,
    )
    partials = exchange(partials.reshape(n_near, 2, far_rows, width), near)
    partials = jnp.sum(partials.astype(F32), axis=0).astype(BF16)
    partials = partials.reshape(2, n_req // 2, n_exp // 4, requests, width)
    partials = partials.transpose(2, 1, 0, 3, 4).reshape(n_far, requests, width)
    partials = exchange(partials, far)
    expert_sum = jnp.sum(partials.astype(F32), axis=0)
    return (stream.astype(F32) + expert_sum).astype(BF16)


def solution(mesh):
    in_specs = (
        P(("req", "exp"), None),
        P(("req", "exp"), "ctx", None, None),
        P(("req", "exp"), "ctx", None, None),
        P(("req", "exp"), "ctx"),
        P(("req", "exp")),
        P(("req", "exp"), None),
        P(),
        P("exp", ("req", "ctx"), None),
        P("exp", ("req", "ctx"), None),
        P("exp", ("req", "ctx"), None),
        P(),
        P(),
        P(),
    )
    out_specs = P(("req", "exp"), "ctx")
    groups = exchange_groups(*(mesh.shape[a] for a in AXES))
    return jax.shard_map(
        functools.partial(on_device, groups),
        mesh=mesh,
        in_specs=in_specs,
        out_specs=out_specs,
        check_vma=False,
    )
```

```python
import functools

import jax
import jax.numpy as jnp
import numpy as np
from jax import lax
from jax.experimental import pallas as pl
from jax.experimental.pallas import tpu as pltpu
from jax.sharding import PartitionSpec as P

HEADS = 48
KV_HEADS = 8
HEAD_DIM = 128
GROUP = HEADS // KV_HEADS
EPSILON = 1e-05
NEGATIVE = -1e30
ROWS = 16
LANES = 128
KERNEL_VMEM = 16 << 20
AXES = ("req", "ctx", "exp")
QUARTERS = ((0, 0), (1, 0), (1, 1), (0, 1))
F32 = jnp.float32
BF16 = jnp.bfloat16


def in_vmem(x):
    return pltpu.with_memory_space_constraint(x, pltpu.VMEM)


def in_hbm(x):
    return pltpu.with_memory_space_constraint(x, pltpu.HBM)


def exchange_groups(n_req, n_ctx, n_exp):
    cols = n_exp // 2

    def device(z, x, y, core):
        z, x, y = (z + core) % n_req, (x + core) % n_ctx, (y + core) % cols
        return (z * n_ctx + x) * n_exp + y * 2 + core

    near = [
        [
            device(2 * zh + zl, 2 * xh + xl, 2 * yh + yl, core)
            for quarter, (zl, yl) in enumerate(QUARTERS)
            for xl in (quarter % 2, 1 - quarter % 2)
        ]
        for core in (0, 1)
        for xh in range(n_ctx // 2)
        for zh in range(n_req // 2)
        for yh in range(cols // 2)
    ]
    far = [
        [
            device(2 * zh + zl, 2 * xh + xl, 2 * yh + yl, core)
            for yh in range(cols // 2)
            for zh in range(n_req // 2)
            for xh in range(n_ctx // 2)
        ]
        for core in (0, 1)
        for xl in (0, 1)
        for zl in (0, 1)
        for yl in (0, 1)
    ]
    columns_far = [
        [
            device(2 * zh + zl, x, 2 * yh + yl, core)
            for zh in range(n_req // 2)
            for yh in range(cols // 2)
        ]
        for core in (0, 1)
        for x in range(n_ctx)
        for zl in (0, 1)
        for yl in (0, 1)
    ]
    return near, far, columns_far


def terms(x):
    first = x.astype(BF16).astype(F32)
    second = (x - first).astype(BF16).astype(F32)
    return [first, second, x - first - second]


def statistic_lanes():
    row = lax.broadcasted_iota(jnp.int32, (ROWS, LANES), 0)
    lane = lax.broadcasted_iota(jnp.int32, (ROWS, LANES), 1)
    return [lane == row + term * ROWS for term in range(6)]


def started(sources, targets, arrived):
    copies = [
        pltpu.make_async_copy(source, target, arrived.at[i])
        for i, (source, target) in enumerate(zip(sources, targets))
    ]
    for copy in copies:
        copy.start()
    return copies


def attention_kernel(n_ctx, *refs):
    sources, (out_ref, own_ref, scale_ref), heads, gains, targets, arrived = (
        refs[:7],
        refs[7:10],
        refs[10],
        refs[11],
        refs[12:19],
        refs[19],
    )
    table, lengths, q_ref, k_ref, v_ref, residual_ref, gain_ref = targets
    copies = started(sources, targets, arrived)
    place = lax.axis_index("ctx")
    requests, slots, page_rows = q_ref.shape[0], k_ref.shape[1], k_ref.shape[2]
    span = table.shape[1]
    positions = slots * page_rows
    heads[...] = jnp.zeros_like(heads)
    for copy in copies[:3]:
        copy.wait()
    queries = q_ref[...].astype(F32)
    for r in range(requests):
        for h in range(HEADS):
            row = (h // GROUP) * ROWS + r * GROUP + h % GROUP
            heads[row : row + 1, :] = queries[r : r + 1, h * HEAD_DIM : (h + 1) * HEAD_DIM]
    at = lax.broadcasted_iota(jnp.int32, (ROWS, positions), 1)
    row_id = lax.broadcasted_iota(jnp.int32, (ROWS, positions), 0)
    slot, offset = at // page_rows, at % page_rows
    live = None
    for r in range(requests):
        seen = None
        for s in range(span):
            position = (s * n_ctx + place) * page_rows + offset
            here = (slot == table[r, s]) & (position < lengths[r])
            seen = here if seen is None else seen | here
        live = seen if live is None else jnp.where(row_id < r * GROUP, live.astype(jnp.int32), seen.astype(jnp.int32)) > 0
    out_row = lax.broadcasted_iota(jnp.int32, (ROWS, LANES), 0)
    places = statistic_lanes()
    live = jnp.concatenate([live] * KV_HEADS, axis=0)
    copies[3].wait()
    keys = k_ref[0].reshape(positions, KV_HEADS * HEAD_DIM)
    query = heads[...].astype(BF16)

    def rows(k):
        return slice(k * ROWS, (k + 1) * ROWS)

    def lanes(k):
        return slice(k * HEAD_DIM, (k + 1) * HEAD_DIM)

    scores = jnp.concatenate(
        [
            lax.dot_general(
                query[rows(k)],
                keys[:, lanes(k)],
                (((1,), (1,)), ((), ())),
                preferred_element_type=F32,
            )
            for k in range(KV_HEADS)
        ],
        axis=0,
    )
    scores = jnp.where(live, scores * HEAD_DIM ** (-0.5), NEGATIVE)
    top = jnp.max(scores, axis=1, keepdims=True)
    weights = jnp.where(live, jnp.exp(scores - top), 0.0)
    total = jnp.sum(weights, axis=1, keepdims=True)
    high = weights.astype(BF16)
    low = (weights - high.astype(F32)).astype(BF16)
    used = requests * GROUP
    copies[4].wait()
    values = v_ref[0].reshape(positions, KV_HEADS * HEAD_DIM)
    for k in range(KV_HEADS):
        mixes = jnp.dot(
            jnp.concatenate([high[rows(k)], low[rows(k)]], axis=0),
            values[:, lanes(k)],
            preferred_element_type=F32,
        )
        mixes = mixes[:ROWS] + mixes[ROWS:]
        statistics = 0.0
        for here, term in zip(places, terms(top[rows(k)]) + terms(total[rows(k)])):
            statistics = jnp.where(here, term, statistics)
        statistics = jnp.sum(statistics, axis=0, keepdims=True)
        part = jnp.where(out_row < used, mixes, statistics).astype(BF16)
        chunk, k = divmod(k, KV_HEADS // n_ctx)
        out_ref[chunk, 0, k] = part
        out_ref[(chunk + n_ctx // 2) % n_ctx, 1, k] = part
    for copy in copies[5:]:
        copy.wait()
    gains[...] = gain_ref[...].astype(F32)
    width = own_ref.shape[2]
    for i in range(2):
        column = lax.rem(place + i * (n_ctx // 2), n_ctx)
        own_ref[i] = residual_ref[:, pl.ds(pl.multiple_of(column * width, width), width)]
        for h in range(width // LANES):
            row = gains[pl.ds(column * (width // LANES) + h, 1), :]
            scale_ref[i, :, h * LANES : (h + 1) * LANES] = row


def attention_parts(
    queries, key_pages, value_pages, block_table, lengths, residual, gain, n_ctx
):
    vmem = pl.BlockSpec(memory_space=pltpu.VMEM)
    scalars, arrays = (block_table, lengths), (queries, key_pages, value_pages, residual, gain)
    return pl.pallas_call(
        functools.partial(attention_kernel, n_ctx),
        out_shape=(
            pltpu.VMEM((n_ctx, 2, KV_HEADS // n_ctx, ROWS, HEAD_DIM), BF16),
            pltpu.VMEM((2, residual.shape[0], residual.shape[1] // n_ctx), BF16),
            pltpu.VMEM((2, 1, residual.shape[1] // n_ctx), F32),
        ),
        in_specs=[pl.BlockSpec(memory_space=pltpu.HBM)] * 7,
        out_specs=(vmem, vmem, vmem),
        scratch_shapes=[pltpu.VMEM((KV_HEADS * ROWS, HEAD_DIM), F32), pltpu.VMEM(gain.shape, F32)]
        + [pltpu.SMEM(x.shape, x.dtype) for x in scalars]
        + [pltpu.VMEM(x.shape, x.dtype) for x in arrays]
        + [pltpu.SemaphoreType.DMA((7,))],
        compiler_params=pltpu.CompilerParams(vmem_limit_bytes=KERNEL_VMEM),
        name="attention_parts",
    )(*(in_hbm(x) for x in scalars + arrays))


def merge_kernel(parts_ref, residual_ref, gain_ref, piece_ref, stream_ref, merged):
    n_src, kv_here = parts_ref.shape[0], parts_ref.shape[2]
    requests, width = stream_ref.shape
    used = requests * GROUP
    place = lax.axis_index("ctx")
    core = lax.rem(lax.axis_index("exp"), 2)
    places = statistic_lanes()
    top_lanes = places[0] | places[1] | places[2]
    total_lanes = places[3] | places[4] | places[5]

    def column(part, lanes):
        row = part[used : used + 1, :]
        return jnp.sum(jnp.where(lanes, row, 0.0), axis=1, keepdims=True)

    scaled, square = [], 0.0
    for i in range(2):
        for k in range(kv_here):
            parts = [parts_ref[s, i, k].astype(F32) for s in range(n_src)]
            tops = [column(part, top_lanes) for part in parts]
            totals = [column(part, total_lanes) for part in parts]
            top = functools.reduce(jnp.maximum, tops)
            scales = [jnp.exp(t - top) for t in tops]
            mixes = sum(parts[s] * scales[s] for s in range(n_src))
            total = sum(totals[s] * scales[s] for s in range(n_src))
            mixes = mixes / total
            for r in range(requests):
                for g in range(GROUP):
                    at = (k * GROUP + g) * HEAD_DIM
                    row = r * GROUP + g
                    merged[i, r : r + 1, at : at + HEAD_DIM] = mixes[row : row + 1, :]
        stream = (residual_ref[i].astype(F32) + merged[i]).astype(BF16)
        if i == 0:
            stream_ref[...] = stream
        wide = stream.astype(F32)
        scaled.append(wide * gain_ref[i])
        square += jnp.sum(wide * wide, axis=1, keepdims=True)
    first, second, third = terms(square)
    lane = lax.broadcasted_iota(jnp.int32, (requests, LANES), 1)
    spread = jnp.where(
        lane == 0, first, jnp.where(lane == 1, second, jnp.where(lane == 2, third, 0.0))
    ).astype(BF16)
    upper = lax.rem(place - core + n_src, n_src) >= n_src // 2
    low = jnp.where(upper, scaled[1], scaled[0]).astype(BF16)
    high = jnp.where(upper, scaled[0], scaled[1]).astype(BF16)
    for copy in range(piece_ref.shape[0]):
        piece_ref[copy, :, :width] = low
        piece_ref[copy, :, width : 2 * width] = high
        piece_ref[copy, :, 2 * width :] = spread


def merge_parts(parts, residual, gain, copies):
    _, requests, width = residual.shape
    vmem = pl.BlockSpec(memory_space=pltpu.VMEM)
    return pl.pallas_call(
        merge_kernel,
        out_shape=(
            pltpu.VMEM((copies, requests, 2 * width + LANES), BF16),
            jax.ShapeDtypeStruct((requests, width), BF16),
        ),
        in_specs=[vmem, vmem, vmem],
        out_specs=(vmem, vmem),
        scratch_shapes=[pltpu.VMEM((2, requests, width), F32)],
        compiler_params=pltpu.CompilerParams(vmem_limit_bytes=KERNEL_VMEM),
        name="merge_parts",
    )(in_vmem(parts), in_vmem(residual), in_vmem(gain))


def row_shares(routes_ref, weights_ref, blocks, core, requests, rows):
    n_exp, _, entries = routes_ref.shape
    n_req, half_y = entries // requests, n_exp // 4
    row = lax.broadcasted_iota(jnp.int32, (entries, rows), 1)
    entry = lax.broadcasted_iota(jnp.int32, (entries, rows), 0)
    request, row = row % requests, row // requests
    yh, row = row % half_y, row // half_y
    zh, row = row % (n_req // 2), row // (n_req // 2)
    zl = sum((row == q).astype(jnp.int32) * QUARTERS[q][0] for q in range(4))
    yl = sum((row == q).astype(jnp.int32) * QUARTERS[q][1] for q in range(4))
    here = entry == (2 * zh + zl + core) % n_req * requests + request
    y = (2 * yh + yl + core) % (n_exp // 2)
    diagonal = lax.broadcasted_iota(jnp.int32, (entries, entries), 0) == lax.broadcasted_iota(
        jnp.int32, (entries, entries), 1
    )
    shares = [jnp.zeros((entries, rows), F32) for _ in blocks]
    for column in range(n_exp // 2):
        routes, weights = routes_ref[2 * column + core], weights_ref[2 * column + core]
        at = here & (y == column)
        for b, block in enumerate(blocks):
            line = jnp.sum(jnp.where(routes == block, weights, 0.0), axis=0, keepdims=True)
            upright = jnp.sum(jnp.where(diagonal, line, 0.0), axis=1, keepdims=True)
            shares[b] += jnp.where(at, upright, 0.0)
    return [jnp.sum(share, axis=0, keepdims=True) for share in shares]


def expert_kernel(model_width, requests, block_source, route_source, weight_source, tokens_ref, *refs):
    sources, gate_held, out_ref, held = refs[:5], refs[5], refs[6], refs[7:12]
    block_expert, routes_ref, weights_ref, turned, arrived = refs[12:]
    copies = started(
        (block_source, route_source, weight_source) + sources,
        (block_expert, routes_ref, weights_ref) + held,
        arrived,
    )
    held = (gate_held,) + held
    for copy in copies[:3]:
        copy.wait()
    copies = copies[3:]
    quarters, n_xl, n_xh, far_rows, width = out_ref.shape
    n_ctx, rows, hidden = n_xl * n_xh, quarters * far_rows, held[0].shape[1]
    contract = (((1,), (1,)), ((), ()))
    ones = jnp.ones((8, LANES), BF16)

    own = lax.axis_index("exp")
    core = lax.rem(own, 2)
    blocks = (block_expert[own + 1 - 2 * core], block_expert[own])
    shares = row_shares(routes_ref, weights_ref, blocks, core, requests, rows)

    def at(chunk):
        column = lax.rem(chunk + n_ctx - core, n_ctx)
        return column % n_xl, column // n_xl

    def own_rows(xl, columns):
        return jnp.concatenate(
            [tokens_ref[q, (xl + q) % n_xl, :, columns] for q in range(quarters)], axis=0
        )

    def added(total, term):
        return term if total is None else total + term

    squares = None
    for xl in range(n_xl):
        tokens = own_rows(xl, slice(n_xh * width, n_xh * width + LANES))
        squares = added(
            squares, lax.dot_general(ones, tokens, contract, preferred_element_type=F32)
        )
        for xh in range(n_xh):
            tokens = own_rows(xl, slice(xh * width, (xh + 1) * width))
            turned[lax.rem(xh * n_xl + xl + core, n_ctx)] = tokens.T
    scale = lax.rsqrt(squares[:1] / model_width + EPSILON)
    active = []
    for b in range(2):
        for copy in copies[1:3] if b else copies[:1]:
            copy.wait()
        products = None
        for chunk in range(n_ctx):
            columns = slice(chunk * width, (chunk + 1) * width)
            wide = jnp.concatenate([w[0, :, columns] for w in held[2 * b : 2 * b + 2]], axis=0)
            products = added(
                products, jnp.dot(wide, turned[chunk], preferred_element_type=F32)
            )
        gate, up = products[:hidden] * scale, products[hidden:] * scale
        active.append(gate / (1.0 + jnp.exp(-gate)) * up * shares[b])
    active.append(jnp.zeros((-2 * hidden % LANES, rows), F32))
    active = jnp.concatenate(active, axis=0).T[:, : 2 * hidden].astype(BF16)
    for copy in copies[3:]:
        copy.wait()
    for chunk in range(n_ctx):
        xl, xh = at(chunk)
        columns = slice(chunk * width, (chunk + 1) * width)
        down = jnp.concatenate([w[0, :, columns] for w in held[4:]], axis=0)
        total = jnp.dot(active, down, preferred_element_type=F32).astype(BF16)
        for q in range(quarters):
            out_ref[q, lax.rem(xl + q, n_xl), xh] = total[q * far_rows : (q + 1) * far_rows]


def expert_partials(
    tokens, routes, route_weights, block_expert, gate_other, weights, requests
):
    quarters, n_xl, far_rows, padded = tokens.shape
    n_xh = 2
    width = (padded - LANES) // n_xh
    rows, model_width = quarters * far_rows, width * n_xl * n_xh
    hidden = weights[0].shape[1]
    hbm = pl.BlockSpec(memory_space=pltpu.HBM)
    vmem = pl.BlockSpec(memory_space=pltpu.VMEM)
    return pl.pallas_call(
        functools.partial(expert_kernel, float(model_width), requests),
        out_shape=pltpu.VMEM((quarters, n_xl, n_xh, far_rows, width), BF16),
        in_specs=[hbm, hbm, hbm, vmem] + [hbm] * len(weights) + [vmem],
        out_specs=vmem,
        scratch_shapes=[pltpu.VMEM(w.shape, w.dtype) for w in weights]
        + [
            pltpu.SMEM(block_expert.shape, block_expert.dtype),
            pltpu.VMEM(routes.shape, routes.dtype),
            pltpu.VMEM(route_weights.shape, route_weights.dtype),
            pltpu.VMEM((n_xl * n_xh, width, rows), BF16),
            pltpu.SemaphoreType.DMA((len(weights) + 3,)),
        ],
        compiler_params=pltpu.CompilerParams(vmem_limit_bytes=KERNEL_VMEM),
        cost_estimate=pl.CostEstimate(
            flops=12 * rows * hidden * model_width,
            bytes_accessed=12 * hidden * model_width,
            transcendentals=0,
        ),
        name="expert_partials",
    )(
        *(in_hbm(x) for x in (block_expert, routes, route_weights)),
        in_vmem(tokens),
        *(in_hbm(w) for w in weights),
        in_vmem(gate_other),
    )


def on_device(
    groups,
    queries,
    key_pages,
    value_pages,
    block_table,
    context_lengths,
    residual,
    norm_gain,
    gate_blocks,
    up_blocks,
    down_blocks,
    expert_routes,
    route_weights,
    block_expert,
):
    near, far, columns_far = groups
    n_req, n_ctx, n_exp = (lax.axis_size(a) for a in AXES)
    requests, model_width = queries.shape
    width = model_width // n_ctx
    n_near, n_far = len(near[0]), len(far[0])
    far_rows = len(columns_far[0]) * requests

    swap = [(i, i ^ 1) for i in range(n_exp)]
    gate_other, up_other, down_other = (
        lax.ppermute(w, "exp", swap) for w in (gate_blocks, up_blocks, down_blocks)
    )

    parts, residual, gain = attention_parts(
        queries,
        key_pages,
        value_pages,
        block_table,
        context_lengths,
        residual,
        norm_gain.reshape(-1, LANES),
        n_ctx,
    )
    parts = lax.all_to_all(parts, "ctx", 0, 0, tiled=True)
    piece, stream = merge_parts(parts, residual, gain, len(columns_far[0]))

    def exchange(x, groups):
        return lax.all_to_all(x, AXES, 0, 0, axis_index_groups=groups, tiled=True)

    tokens = exchange(piece, columns_far)
    tokens = tokens.reshape(far_rows, piece.shape[2])
    tokens = exchange(jnp.broadcast_to(tokens, (n_near,) + tokens.shape), near)
    tokens = tokens.reshape(n_near // 2, 2, far_rows, piece.shape[2])
    partials = expert_partials(
        tokens,
        expert_routes.transpose(0, 2, 1),
        route_weights.transpose(0, 2, 1),
        block_expert,
        gate_other,
        (up_other, gate_blocks, up_blocks, down_other, down_blocks),
        requests,
    )
    partials = exchange(partials.reshape(n_near, 2, far_rows, width), near)
    partials = jnp.sum(partials.astype(F32), axis=0).astype(BF16)
    partials = partials.reshape(2, n_req // 2, n_exp // 4, requests, width)
    partials = partials.transpose(2, 1, 0, 3, 4).reshape(n_far, requests, width)
    partials = exchange(partials, far)
    expert_sum = jnp.sum(partials.astype(F32), axis=0)
    return (stream.astype(F32) + expert_sum).astype(BF16)


def solution(mesh):
    in_specs = (
        P(("req", "exp"), None),
        P(("req", "exp"), "ctx", None, None),
        P(("req", "exp"), "ctx", None, None),
        P(("req", "exp"), "ctx"),
        P(("req", "exp")),
        P(("req", "exp"), None),
        P(),
        P("exp", ("req", "ctx"), None),
        P("exp", ("req", "ctx"), None),
        P("exp", ("req", "ctx"), None),
        P(),
        P(),
        P(),
    )
    out_specs = P(("req", "exp"), "ctx")
    groups = exchange_groups(*(mesh.shape[a] for a in AXES))
    return jax.shard_map(
        functools.partial(on_device, groups),
        mesh=mesh,
        in_specs=in_specs,
        out_specs=out_specs,
        check_vma=False,
    )
```

```python
import functools

import jax
import jax.numpy as jnp
import numpy as np
from jax import lax
from jax.experimental import pallas as pl
from jax.experimental.pallas import tpu as pltpu
from jax.sharding import PartitionSpec as P

HEADS = 48
KV_HEADS = 8
HEAD_DIM = 128
GROUP = HEADS // KV_HEADS
EPSILON = 1e-05
NEGATIVE = -1e30
ROWS = 16
LANES = 128
KERNEL_VMEM = 16 << 20
AXES = ("req", "ctx", "exp")
QUARTERS = ((0, 0), (1, 0), (1, 1), (0, 1))
F32 = jnp.float32
BF16 = jnp.bfloat16


def in_vmem(x):
    return pltpu.with_memory_space_constraint(x, pltpu.VMEM)


def in_hbm(x):
    return pltpu.with_memory_space_constraint(x, pltpu.HBM)


def exchange_groups(n_req, n_ctx, n_exp):
    cols = n_exp // 2

    def device(z, x, y, core):
        z, x, y = (z + core) % n_req, (x + core) % n_ctx, (y + core) % cols
        return (z * n_ctx + x) * n_exp + y * 2 + core

    near = [
        [
            device(2 * zh + zl, 2 * xh + xl, 2 * yh + yl, core)
            for quarter, (zl, yl) in enumerate(QUARTERS)
            for xl in (quarter % 2, 1 - quarter % 2)
        ]
        for core in (0, 1)
        for xh in range(n_ctx // 2)
        for zh in range(n_req // 2)
        for yh in range(cols // 2)
    ]
    far = [
        [
            device(2 * zh + zl, 2 * xh + xl, 2 * yh + yl, core)
            for yh in range(cols // 2)
            for zh in range(n_req // 2)
            for xh in range(n_ctx // 2)
        ]
        for core in (0, 1)
        for xl in (0, 1)
        for zl in (0, 1)
        for yl in (0, 1)
    ]
    columns_far = [
        [
            device(2 * zh + zl, x, 2 * yh + yl, core)
            for zh in range(n_req // 2)
            for yh in range(cols // 2)
        ]
        for core in (0, 1)
        for x in range(n_ctx)
        for zl in (0, 1)
        for yl in (0, 1)
    ]
    return near, far, columns_far


def started(sources, targets, arrived):
    copies = [
        pltpu.make_async_copy(source, target, arrived.at[i])
        for i, (source, target) in enumerate(zip(sources, targets))
    ]
    for copy in copies:
        copy.start()
    return copies


def attention_kernel(n_ctx, *refs):
    sources, (out_ref, own_ref, scale_ref), heads, gains, targets, arrived = (
        refs[:7],
        refs[7:10],
        refs[10],
        refs[11],
        refs[12:19],
        refs[19],
    )
    table, lengths, q_ref, k_ref, v_ref, residual_ref, gain_ref = targets
    copies = started(sources, targets, arrived)
    place = lax.axis_index("ctx")
    requests, slots, page_rows = q_ref.shape[0], k_ref.shape[1], k_ref.shape[2]
    span = table.shape[1]
    positions = slots * page_rows
    heads[...] = jnp.zeros_like(heads)
    for copy in copies[:3]:
        copy.wait()
    queries = q_ref[...].astype(F32)
    for r in range(requests):
        for h in range(HEADS):
            row = (h // GROUP) * ROWS + r * GROUP + h % GROUP
            heads[row : row + 1, :] = queries[r : r + 1, h * HEAD_DIM : (h + 1) * HEAD_DIM]
    at = lax.broadcasted_iota(jnp.int32, (ROWS, positions), 1)
    row_id = lax.broadcasted_iota(jnp.int32, (ROWS, positions), 0)
    slot, offset = at // page_rows, at % page_rows
    live = None
    for r in range(requests):
        seen = None
        for s in range(span):
            position = (s * n_ctx + place) * page_rows + offset
            here = (slot == table[r, s]) & (position < lengths[r])
            seen = here if seen is None else seen | here
        live = seen if live is None else jnp.where(row_id < r * GROUP, live.astype(jnp.int32), seen.astype(jnp.int32)) > 0
    out_row = lax.broadcasted_iota(jnp.int32, (ROWS, LANES), 0)
    diagonal = out_row == lax.broadcasted_iota(jnp.int32, (ROWS, LANES), 1)
    live = jnp.concatenate([live] * KV_HEADS, axis=0)
    copies[3].wait()
    keys = k_ref[0].reshape(positions, KV_HEADS * HEAD_DIM)
    query = heads[...].astype(BF16)

    def rows(k):
        return slice(k * ROWS, (k + 1) * ROWS)

    def lanes(k):
        return slice(k * HEAD_DIM, (k + 1) * HEAD_DIM)

    scores = jnp.concatenate(
        [
            lax.dot_general(
                query[rows(k)],
                keys[:, lanes(k)],
                (((1,), (1,)), ((), ())),
                preferred_element_type=F32,
            )
            for k in range(KV_HEADS)
        ],
        axis=0,
    )
    scores = jnp.where(live, scores * HEAD_DIM ** (-0.5), NEGATIVE)
    top = jnp.max(scores, axis=1, keepdims=True)
    weights = jnp.where(live, jnp.exp(scores - top), 0.0)
    total = jnp.sum(weights, axis=1, keepdims=True)
    high = weights.astype(BF16)
    low = (weights - high.astype(F32)).astype(BF16)
    used = requests * GROUP
    copies[4].wait()
    values = v_ref[0].reshape(positions, KV_HEADS * HEAD_DIM)
    for k in range(KV_HEADS):
        mixes = jnp.dot(
            jnp.concatenate([high[rows(k)], low[rows(k)]], axis=0),
            values[:, lanes(k)],
            preferred_element_type=F32,
        )
        mixes = mixes[:ROWS] + mixes[ROWS:]
        top_row = jnp.sum(jnp.where(diagonal, top[rows(k)], 0.0), axis=0, keepdims=True)
        total_row = jnp.sum(jnp.where(diagonal, total[rows(k)], 0.0), axis=0, keepdims=True)
        part = jnp.where(
            out_row < used, mixes, jnp.where(out_row == used, top_row, total_row)
        )
        chunk, k = divmod(k, KV_HEADS // n_ctx)
        out_ref[chunk, 0, k] = part
        out_ref[(chunk + n_ctx // 2) % n_ctx, 1, k] = part
    for copy in copies[5:]:
        copy.wait()
    gains[...] = gain_ref[...].astype(F32)
    width = own_ref.shape[2]
    for i in range(2):
        column = lax.rem(place + i * (n_ctx // 2), n_ctx)
        own_ref[i] = residual_ref[:, pl.ds(pl.multiple_of(column * width, width), width)]
        for h in range(width // LANES):
            row = gains[pl.ds(column * (width // LANES) + h, 1), :]
            scale_ref[i, :, h * LANES : (h + 1) * LANES] = row


def attention_parts(
    queries, key_pages, value_pages, block_table, lengths, residual, gain, n_ctx
):
    vmem = pl.BlockSpec(memory_space=pltpu.VMEM)
    scalars, arrays = (block_table, lengths), (queries, key_pages, value_pages, residual, gain)
    return pl.pallas_call(
        functools.partial(attention_kernel, n_ctx),
        out_shape=(
            pltpu.VMEM((n_ctx, 2, KV_HEADS // n_ctx, ROWS, HEAD_DIM), F32),
            pltpu.VMEM((2, residual.shape[0], residual.shape[1] // n_ctx), BF16),
            pltpu.VMEM((2, 1, residual.shape[1] // n_ctx), F32),
        ),
        in_specs=[pl.BlockSpec(memory_space=pltpu.HBM)] * 7,
        out_specs=(vmem, vmem, vmem),
        scratch_shapes=[pltpu.VMEM((KV_HEADS * ROWS, HEAD_DIM), F32), pltpu.VMEM(gain.shape, F32)]
        + [pltpu.SMEM(x.shape, x.dtype) for x in scalars]
        + [pltpu.VMEM(x.shape, x.dtype) for x in arrays]
        + [pltpu.SemaphoreType.DMA((7,))],
        compiler_params=pltpu.CompilerParams(vmem_limit_bytes=KERNEL_VMEM),
        name="attention_parts",
    )(*(in_hbm(x) for x in scalars + arrays))


def merge_kernel(parts_ref, residual_ref, gain_ref, piece_ref, stream_ref, merged):
    n_src, kv_here = parts_ref.shape[0], parts_ref.shape[2]
    requests, width = stream_ref.shape
    used = requests * GROUP
    place = lax.axis_index("ctx")
    core = lax.rem(lax.axis_index("exp"), 2)
    diagonal = lax.broadcasted_iota(jnp.int32, (ROWS, LANES), 0) == lax.broadcasted_iota(
        jnp.int32, (ROWS, LANES), 1
    )

    def column(row):
        return jnp.sum(jnp.where(diagonal, row, 0.0), axis=1, keepdims=True)

    scaled, square = [], 0.0
    for i in range(2):
        for k in range(kv_here):
            tops = [column(parts_ref[s, i, k, used : used + 1, :]) for s in range(n_src)]
            totals = [column(parts_ref[s, i, k, used + 1 : used + 2, :]) for s in range(n_src)]
            top = functools.reduce(jnp.maximum, tops)
            scales = [jnp.exp(t - top) for t in tops]
            mixes = sum(parts_ref[s, i, k] * scales[s] for s in range(n_src))
            total = sum(totals[s] * scales[s] for s in range(n_src))
            mixes = mixes / total
            for r in range(requests):
                for g in range(GROUP):
                    at = (k * GROUP + g) * HEAD_DIM
                    row = r * GROUP + g
                    merged[i, r : r + 1, at : at + HEAD_DIM] = mixes[row : row + 1, :]
        stream = (residual_ref[i].astype(F32) + merged[i]).astype(BF16)
        if i == 0:
            stream_ref[...] = stream
        wide = stream.astype(F32)
        scaled.append(wide * gain_ref[i])
        square += jnp.sum(wide * wide, axis=1, keepdims=True)
    first = square.astype(BF16).astype(F32)
    second = (square - first).astype(BF16).astype(F32)
    third = square - first - second
    lane = lax.broadcasted_iota(jnp.int32, (requests, LANES), 1)
    spread = jnp.where(
        lane == 0, first, jnp.where(lane == 1, second, jnp.where(lane == 2, third, 0.0))
    ).astype(BF16)
    upper = lax.rem(place - core + n_src, n_src) >= n_src // 2
    low = jnp.where(upper, scaled[1], scaled[0]).astype(BF16)
    high = jnp.where(upper, scaled[0], scaled[1]).astype(BF16)
    for copy in range(piece_ref.shape[0]):
        piece_ref[copy, :, :width] = low
        piece_ref[copy, :, width : 2 * width] = high
        piece_ref[copy, :, 2 * width :] = spread


def merge_parts(parts, residual, gain, copies):
    _, requests, width = residual.shape
    vmem = pl.BlockSpec(memory_space=pltpu.VMEM)
    return pl.pallas_call(
        merge_kernel,
        out_shape=(
            pltpu.VMEM((copies, requests, 2 * width + LANES), BF16),
            jax.ShapeDtypeStruct((requests, width), BF16),
        ),
        in_specs=[vmem, vmem, vmem],
        out_specs=(vmem, vmem),
        scratch_shapes=[pltpu.VMEM((2, requests, width), F32)],
        compiler_params=pltpu.CompilerParams(vmem_limit_bytes=KERNEL_VMEM),
        name="merge_parts",
    )(in_vmem(parts), in_vmem(residual), in_vmem(gain))


def row_shares(routes_ref, weights_ref, blocks, core, requests, rows):
    n_exp, _, entries = routes_ref.shape
    n_req, half_y = entries // requests, n_exp // 4
    row = lax.broadcasted_iota(jnp.int32, (entries, rows), 1)
    entry = lax.broadcasted_iota(jnp.int32, (entries, rows), 0)
    request, row = row % requests, row // requests
    yh, row = row % half_y, row // half_y
    zh, row = row % (n_req // 2), row // (n_req // 2)
    zl = sum((row == q).astype(jnp.int32) * QUARTERS[q][0] for q in range(4))
    yl = sum((row == q).astype(jnp.int32) * QUARTERS[q][1] for q in range(4))
    here = entry == (2 * zh + zl + core) % n_req * requests + request
    y = (2 * yh + yl + core) % (n_exp // 2)
    diagonal = lax.broadcasted_iota(jnp.int32, (entries, entries), 0) == lax.broadcasted_iota(
        jnp.int32, (entries, entries), 1
    )
    shares = [jnp.zeros((entries, rows), F32) for _ in blocks]
    for column in range(n_exp // 2):
        routes, weights = routes_ref[2 * column + core], weights_ref[2 * column + core]
        at = here & (y == column)
        for b, block in enumerate(blocks):
            line = jnp.sum(jnp.where(routes == block, weights, 0.0), axis=0, keepdims=True)
            upright = jnp.sum(jnp.where(diagonal, line, 0.0), axis=1, keepdims=True)
            shares[b] += jnp.where(at, upright, 0.0)
    return [jnp.sum(share, axis=0, keepdims=True) for share in shares]


def expert_kernel(model_width, requests, block_source, route_source, weight_source, tokens_ref, *refs):
    sources, gate_held, out_ref, held = refs[:5], refs[5], refs[6], refs[7:12]
    block_expert, routes_ref, weights_ref, turned, arrived = refs[12:]
    copies = started(
        (block_source, route_source, weight_source) + sources,
        (block_expert, routes_ref, weights_ref) + held,
        arrived,
    )
    held = (gate_held,) + held
    for copy in copies[:3]:
        copy.wait()
    copies = copies[3:]
    quarters, n_xl, n_xh, far_rows, width = out_ref.shape
    n_ctx, rows, hidden = n_xl * n_xh, quarters * far_rows, held[0].shape[1]
    contract = (((1,), (1,)), ((), ()))
    ones = jnp.ones((8, LANES), BF16)

    own = lax.axis_index("exp")
    core = lax.rem(own, 2)
    blocks = (block_expert[own + 1 - 2 * core], block_expert[own])
    shares = row_shares(routes_ref, weights_ref, blocks, core, requests, rows)

    def at(chunk):
        column = lax.rem(chunk + n_ctx - core, n_ctx)
        return column % n_xl, column // n_xl

    def own_rows(xl, columns):
        return jnp.concatenate(
            [tokens_ref[q, (xl + q) % n_xl, :, columns] for q in range(quarters)], axis=0
        )

    def added(total, term):
        return term if total is None else total + term

    squares = None
    for xl in range(n_xl):
        tokens = own_rows(xl, slice(n_xh * width, n_xh * width + LANES))
        squares = added(
            squares, lax.dot_general(ones, tokens, contract, preferred_element_type=F32)
        )
        for xh in range(n_xh):
            tokens = own_rows(xl, slice(xh * width, (xh + 1) * width))
            turned[lax.rem(xh * n_xl + xl + core, n_ctx)] = tokens.T
    scale = lax.rsqrt(squares[:1] / model_width + EPSILON)
    active = []
    for b in range(2):
        for copy in copies[1:3] if b else copies[:1]:
            copy.wait()
        products = None
        for chunk in range(n_ctx):
            columns = slice(chunk * width, (chunk + 1) * width)
            wide = jnp.concatenate([w[0, :, columns] for w in held[2 * b : 2 * b + 2]], axis=0)
            products = added(
                products, jnp.dot(wide, turned[chunk], preferred_element_type=F32)
            )
        gate, up = products[:hidden] * scale, products[hidden:] * scale
        active.append(gate / (1.0 + jnp.exp(-gate)) * up * shares[b])
    active.append(jnp.zeros((-2 * hidden % LANES, rows), F32))
    active = jnp.concatenate(active, axis=0).T[:, : 2 * hidden].astype(BF16)
    for copy in copies[3:]:
        copy.wait()
    for chunk in range(n_ctx):
        xl, xh = at(chunk)
        columns = slice(chunk * width, (chunk + 1) * width)
        down = jnp.concatenate([w[0, :, columns] for w in held[4:]], axis=0)
        total = jnp.dot(active, down, preferred_element_type=F32).astype(BF16)
        for q in range(quarters):
            out_ref[q, lax.rem(xl + q, n_xl), xh] = total[q * far_rows : (q + 1) * far_rows]


def expert_partials(
    tokens, routes, route_weights, block_expert, gate_other, weights, requests
):
    quarters, n_xl, far_rows, padded = tokens.shape
    n_xh = 2
    width = (padded - LANES) // n_xh
    rows, model_width = quarters * far_rows, width * n_xl * n_xh
    hidden = weights[0].shape[1]
    hbm = pl.BlockSpec(memory_space=pltpu.HBM)
    vmem = pl.BlockSpec(memory_space=pltpu.VMEM)
    return pl.pallas_call(
        functools.partial(expert_kernel, float(model_width), requests),
        out_shape=pltpu.VMEM((quarters, n_xl, n_xh, far_rows, width), BF16),
        in_specs=[hbm, hbm, hbm, vmem] + [hbm] * len(weights) + [vmem],
        out_specs=vmem,
        scratch_shapes=[pltpu.VMEM(w.shape, w.dtype) for w in weights]
        + [
            pltpu.SMEM(block_expert.shape, block_expert.dtype),
            pltpu.VMEM(routes.shape, routes.dtype),
            pltpu.VMEM(route_weights.shape, route_weights.dtype),
            pltpu.VMEM((n_xl * n_xh, width, rows), BF16),
            pltpu.SemaphoreType.DMA((len(weights) + 3,)),
        ],
        compiler_params=pltpu.CompilerParams(vmem_limit_bytes=KERNEL_VMEM),
        cost_estimate=pl.CostEstimate(
            flops=12 * rows * hidden * model_width,
            bytes_accessed=12 * hidden * model_width,
            transcendentals=0,
        ),
        name="expert_partials",
    )(
        *(in_hbm(x) for x in (block_expert, routes, route_weights)),
        in_vmem(tokens),
        *(in_hbm(w) for w in weights),
        in_vmem(gate_other),
    )


def near_sum_kernel(half_y, parts_ref, out_ref):
    n_near, n_xh, far_rows, _ = parts_ref.shape
    n_far, requests, _ = out_ref.shape
    half_z = n_far // n_xh // half_y
    for xh in range(n_xh):
        total = parts_ref[0, xh].astype(F32)
        for p in range(1, n_near):
            total += parts_ref[p, xh].astype(F32)
        for zh in range(half_z):
            for yh in range(half_y):
                row = (zh * half_y + yh) * requests
                out_ref[(yh * half_z + zh) * n_xh + xh] = total[row : row + requests].astype(BF16)


def near_sum(parts, n_far, half_y):
    _, n_xh, far_rows, width = parts.shape
    vmem = pl.BlockSpec(memory_space=pltpu.VMEM)
    return pl.pallas_call(
        functools.partial(near_sum_kernel, half_y),
        out_shape=pltpu.VMEM((n_far, n_xh * far_rows // n_far, width), BF16),
        in_specs=[vmem],
        out_specs=vmem,
        compiler_params=pltpu.CompilerParams(vmem_limit_bytes=KERNEL_VMEM),
        name="near_sum",
    )(in_vmem(parts))


def on_device(
    groups,
    queries,
    key_pages,
    value_pages,
    block_table,
    context_lengths,
    residual,
    norm_gain,
    gate_blocks,
    up_blocks,
    down_blocks,
    expert_routes,
    route_weights,
    block_expert,
):
    near, far, columns_far = groups
    n_req, n_ctx, n_exp = (lax.axis_size(a) for a in AXES)
    requests, model_width = queries.shape
    width = model_width // n_ctx
    n_near, n_far = len(near[0]), len(far[0])
    far_rows = len(columns_far[0]) * requests

    swap = [(i, i ^ 1) for i in range(n_exp)]
    gate_other, up_other, down_other = (
        lax.ppermute(w, "exp", swap) for w in (gate_blocks, up_blocks, down_blocks)
    )

    parts, residual, gain = attention_parts(
        queries,
        key_pages,
        value_pages,
        block_table,
        context_lengths,
        residual,
        norm_gain.reshape(-1, LANES),
        n_ctx,
    )
    parts = lax.all_to_all(parts, "ctx", 0, 0, tiled=True)
    piece, stream = merge_parts(parts, residual, gain, len(columns_far[0]))

    def exchange(x, groups):
        return lax.all_to_all(x, AXES, 0, 0, axis_index_groups=groups, tiled=True)

    tokens = exchange(piece, columns_far)
    tokens = tokens.reshape(far_rows, piece.shape[2])
    tokens = exchange(jnp.broadcast_to(tokens, (n_near,) + tokens.shape), near)
    tokens = tokens.reshape(n_near // 2, 2, far_rows, piece.shape[2])
    partials = expert_partials(
        tokens,
        expert_routes.transpose(0, 2, 1),
        route_weights.transpose(0, 2, 1),
        block_expert,
        gate_other,
        (up_other, gate_blocks, up_blocks, down_other, down_blocks),
        requests,
    )
    partials = exchange(partials.reshape(n_near, 2, far_rows, width), near)
    partials = near_sum(partials, n_far, n_exp // 4)
    partials = exchange(partials, far)
    expert_sum = jnp.sum(partials.astype(F32), axis=0)
    return (stream.astype(F32) + expert_sum).astype(BF16)


def solution(mesh):
    in_specs = (
        P(("req", "exp"), None),
        P(("req", "exp"), "ctx", None, None),
        P(("req", "exp"), "ctx", None, None),
        P(("req", "exp"), "ctx"),
        P(("req", "exp")),
        P(("req", "exp"), None),
        P(),
        P("exp", ("req", "ctx"), None),
        P("exp", ("req", "ctx"), None),
        P("exp", ("req", "ctx"), None),
        P(),
        P(),
        P(),
    )
    out_specs = P(("req", "exp"), "ctx")
    groups = exchange_groups(*(mesh.shape[a] for a in AXES))
    return jax.shard_map(
        functools.partial(on_device, groups),
        mesh=mesh,
        in_specs=in_specs,
        out_specs=out_specs,
        check_vma=False,
    )
```
